1024 devices in a mesh: dp: 32 (over x, z_hi, y), mp: 32 (over z_lo, core).
Axes of the slice: x: 4, y: 4, z: 32 (z_hi: 2, z_lo: 16; z = z_hi * 16 + z_lo), core: 2. Of those that a mesh axis runs over, the one named last changes fastest.
Arguments:
- image_emb: float32 [4096, 1152], P('dp', 'mp'), may hold values from -0.8 to 0.8
- text_emb: float32 [4096, 1152], P('dp', 'mp'), may hold values from -0.8 to 0.8
- log_scale: float32 [1], replicated, may hold values from 0 to 1
- logit_bias: float32 [1], replicated, may hold values from -6 to -4
Outputs:
- grad_image: float32 [4096, 1152], P('dp', 'mp')
- grad_text: float32 [4096, 1152], P('dp', 'mp')
The draws below stay inside these ranges and needn't reach their ends.
All inputs are finite; a program needn't handle non-finite values.
Results may differ from the reference program's by a relative error of at most 0.00007.
Values sent between devices are 32-bit elements; how exact they have to be, the bound alone decides.
No kernel may reach another device: no remote copies, remote signals or barrier semaphores. Data moves between devices by JAX's collectives and lax.ppermute only.
A program may use at most 32 MiB of HBM per device.

```python
import jax
import jax.numpy as jnp
from jax import lax

D = 1152
PAIRS = 4096


def level_of(key, shape, split, smallest, largest):
    level = 1.0
    for position, parts in split:
        heights = jax.random.uniform(jax.random.fold_in(jax.random.fold_in(key, 6), position), (parts,), jnp.float32, smallest / len(split), largest / len(split))
        level = level * jnp.repeat(jnp.exp(heights), shape[position] // parts).reshape((-1,) + (1,) * (len(shape) - 1 - position))
    return level


def noise(rng, extent, width, most, cuts=(), kind=jnp.bfloat16):
    loudness = level_of(rng, extent, cuts, -0.22, 0.18) if cuts else 1.0
    values = jax.random.normal(rng, extent, jnp.float32) * width * loudness
    return jnp.minimum(jnp.maximum(values, -most), most).astype(kind)


def setup_inputs(seed: int = 0) -> dict:
    keys = jax.random.split(jax.random.key(seed), 5)
    return {
        "image_emb": noise(keys[0], (PAIRS, D), 0.108, 0.8, ((0, 32), (1, 32)), jnp.float32),
        "text_emb": noise(keys[1], (PAIRS, D), 0.108, 0.8, ((0, 32), (1, 32)), jnp.float32),
        "log_scale": jnp.clip(jax.random.uniform(keys[2], (1,), jnp.float32, 0.0, 1.0), 0.0, 1.0),
        "logit_bias": jnp.clip(jax.random.uniform(keys[3], (1,), jnp.float32, -6.0, -4.0), -6.0, -4.0),
    }


def reference(image_emb, text_emb, log_scale, logit_bias):
    scale = jnp.exp(log_scale[0])
    logits = scale * jnp.dot(image_emb, text_emb.T, preferred_element_type=jnp.float32, precision=lax.Precision.HIGHEST) + logit_bias[0]
    count = image_emb.shape[0]
    label = 2.0 * jnp.eye(count, dtype=jnp.float32) - 1.0
    coef = -label * jax.nn.sigmoid(-label * logits)
    grad_image = scale * jnp.dot(coef, text_emb, preferred_element_type=jnp.float32, precision=lax.Precision.HIGHEST)
    grad_text = scale * jnp.dot(coef.T, image_emb, preferred_element_type=jnp.float32, precision=lax.Precision.HIGHEST)
    return grad_image, grad_text
```

```python
import functools

import jax
import jax.numpy as jnp
from jax import lax
from jax.experimental import pallas as pl
from jax.experimental.pallas import tpu as pltpu
from jax.sharding import Mesh, PartitionSpec as P

LANES = 128
VMEM = pl.BlockSpec(memory_space=pltpu.VMEM)
SMEM = pl.BlockSpec(memory_space=pltpu.SMEM)


def rows_first(block):
    narrow, rows = block.shape
    filled = jnp.concatenate([block, jnp.zeros((LANES - narrow, rows), block.dtype)], axis=0)
    return filled.T


def only(block, width):
    lane = lax.broadcasted_iota(jnp.int32, block.shape, 1)
    return jnp.where(lane < width, block, 0.0)


def shift(block, lanes):
    lanes = lanes % LANES
    return block if lanes == 0 else pltpu.roll(block, lanes, 1)


def split_kernel(sizes, image_ref, text_ref, out_ref):
    high, low, of_i, of_j = sizes
    narrow, rows = image_ref.shape
    image, text = rows_first(image_ref[...]), rows_first(text_ref[...])
    group, small = rows // of_i, rows // of_j
    halves = group // small
    near = low // of_i
    images = []
    for i in range(of_i):
        total = None
        for h in range(halves):
            start = i * group + h * small
            part = shift(image[start : start + small], h * narrow)
            total = part if total is None else total + part
        images.append(total)
    texts = [shift(text[j * small : (j + 1) * small], halves * narrow) for j in range(of_j)]
    for zh in range(high):
        for zl in range(low):
            out_ref[zh * low + zl] = images[zl // near] + texts[zh * near + zl % near]


def widen_kernel(sizes, narrow, got_ref, image_ref, text_ref):
    high, low, halves = sizes
    small = got_ref.shape[1]
    copies_i, copies_t = image_ref.shape[0], text_ref.shape[0]
    tiles = -(-low * narrow // LANES)
    for zh in range(high):
        for h in range(halves + 1):
            acc = [None] * tiles
            for zl in range(low):
                part = got_ref[zh * low + zl]
                lane = lax.broadcasted_iota(jnp.int32, part.shape, 1)
                tile, at = divmod(zl * narrow, LANES)
                moved = shift(part, at - h * narrow)
                end = at + narrow
                mine = jnp.where((lane >= at) & (lane < end), moved, 0.0)
                acc[tile] = mine if acc[tile] is None else acc[tile] + mine
                if end > LANES:
                    mine = jnp.where(lane < end - LANES, moved, 0.0)
                    acc[tile + 1] = mine
            for tile in range(tiles):
                lo = tile * LANES
                hi = min(lo + LANES, low * narrow)
                value = acc[tile][:, : hi - lo]
                if h < halves:
                    at = (zh * halves + h) * small
                    for k in range(copies_i):
                        image_ref[k, at : at + small, lo:hi] = value
                else:
                    for k in range(copies_t):
                        text_ref[k, zh * small : (zh + 1) * small, lo:hi] = value


def logits_kernel(image_ref, text_ref, out_ref):
    a, m, w = image_ref.shape
    b, n, _ = text_ref.shape
    out_ref[...] = lax.dot_general(
        image_ref[...].reshape(a * m, w),
        text_ref[...].reshape(b * n, w),
        (((1,), (1,)), ((), ())),
        preferred_element_type=jnp.float32,
        precision=lax.Precision.HIGHEST,
    )


def grads_kernel(sizes, at_ref, log_scale_ref, bias_ref, mine_ref, other_ref, image_ref, text_ref, gi_ref, gt_ref):
    high, halves, small, rows, of_y = sizes
    a, m, w = image_ref.shape
    b, n, _ = text_ref.shape
    scale = jnp.exp(jnp.full((1, 1), log_scale_ref[0], jnp.float32))
    logits = scale * (mine_ref[...] + other_ref[...]) + bias_ref[0]
    x, y, i, j = at_ref[0], at_ref[1], at_ref[2], at_ref[3]
    r = lax.broadcasted_iota(jnp.int32, logits.shape, 0)
    yy, zh, inner = r // m, (r % m) // (halves * small), r % (halves * small)
    row_ids = (x * high * of_y + zh * of_y + yy) * rows + i * (halves * small) + inner
    c = lax.broadcasted_iota(jnp.int32, logits.shape, 1)
    xx, zh, inner = c // n, (c % n) // small, c % small
    col_ids = (xx * high * of_y + zh * of_y + y) * rows + j * small + inner
    label = jnp.where(row_ids == col_ids, 1.0, -1.0)
    coef = -label * jax.nn.sigmoid(-label * logits)
    image = image_ref[...].reshape(a * m, w)
    text = text_ref[...].reshape(b * n, w)
    dot = functools.partial(
        lax.dot_general, preferred_element_type=jnp.float32, precision=lax.Precision.HIGHEST
    )
    gi_ref[...] = (scale * dot(coef, text, (((1,), (0,)), ((), ())))).reshape(a, m, w)
    gt_ref[...] = (scale * dot(coef, image, (((0,), (0,)), ((), ())))).reshape(b, n, w)


def narrow_kernel(sizes, narrow, image_ref, text_ref, out_ref):
    high, low, halves = sizes
    small = out_ref.shape[1]
    tiles = -(-low * narrow // LANES)
    width = low * narrow

    def summed(ref, start):
        found = []
        for tile in range(tiles):
            lo = tile * LANES
            hi = min(lo + LANES, width)
            value = ref[0, start : start + small, lo:hi]
            for k in range(1, ref.shape[0]):
                value = value + ref[k, start : start + small, lo:hi]
            if hi - lo < LANES:
                value = jnp.concatenate([value, jnp.zeros((small, LANES - hi + lo), value.dtype)], axis=1)
            found.append(value)
        return found

    for zh in range(high):
        sums = [summed(image_ref, (zh * halves + h) * small) for h in range(halves)]
        sums.append(summed(text_ref, zh * small))
        for zl in range(low):
            tile, at = divmod(zl * narrow, LANES)
            total = None
            for h, value in enumerate(sums):
                lane = lax.broadcasted_iota(jnp.int32, value[0].shape, 1)
                to = h * narrow
                moved = shift(value[tile], to - at)
                here = min(narrow, LANES - at)
                part = jnp.where((lane >= to) & (lane < to + here), moved, 0.0)
                if here < narrow:
                    moved = shift(value[tile + 1], to - at)
                    part = part + jnp.where((lane >= to + here) & (lane < to + narrow), moved, 0.0)
                total = part if total is None else total + part
            out_ref[zh * low + zl] = total


def collect_kernel(sizes, got_ref, image_ref, text_ref):
    high, low, of_i, of_j = sizes
    narrow, rows = image_ref.shape
    small = got_ref.shape[1]
    group = rows // of_i
    halves = group // small
    near = low // of_i

    def total(sources):
        value = got_ref[sources[0]]
        for source in sources[1:]:
            value = value + got_ref[source]
        return value

    images = []
    for i in range(of_i):
        value = total([zh * low + i * near + k for zh in range(high) for k in range(near)])
        for h in range(halves):
            images.append(shift(value, -h * narrow))
    texts = []
    for j in range(of_j):
        zh, k = divmod(j, near)
        texts.append(shift(total([zh * low + i * near + k for i in range(of_i)]), -halves * narrow))
    image_ref[...] = jnp.concatenate(images, axis=0).T[:narrow]
    text_ref[...] = jnp.concatenate(texts, axis=0).T[:narrow]


def call(kernel, outs, *operands, scalars=0):
    many = isinstance(outs, list)
    shapes = [jax.ShapeDtypeStruct(s, jnp.float32) for s in (outs if many else [outs])]
    return pl.pallas_call(
        kernel,
        out_shape=shapes if many else shapes[0],
        in_specs=[SMEM] * scalars + [VMEM] * (len(operands) - scalars),
        out_specs=[VMEM] * len(shapes) if many else VMEM,
        compiler_params=pltpu.CompilerParams(vmem_limit_bytes=32 * 1024 * 1024),
    )(*operands)


def exchange(value, axis):
    return lax.all_to_all(value, axis, split_axis=0, concat_axis=0, tiled=True)


def on_device(image_emb, text_emb, log_scale, logit_bias):
    of_x, high, of_y, low = (lax.axis_size(a) for a in ("x", "zh", "y", "zl"))
    rows, narrow = image_emb.shape
    of_i = {16: 4, 4: 2}[low]
    near = low // of_i
    of_j = high * near
    group, small = rows // of_i, rows // of_j
    halves = group // small
    wide = low * narrow
    place = (high, low, of_i, of_j)
    inner = (high, low, halves)

    sent = call(functools.partial(split_kernel, place), (high * low, small, LANES), image_emb.T, text_emb.T)
    got = exchange(sent, ("zh", "zl"))
    mine_i, mine_t = call(
        functools.partial(widen_kernel, inner, narrow),
        [(of_y, high * group, wide), (of_x, high * small, wide)],
        got,
    )
    image = exchange(mine_i, "y")
    text = exchange(mine_t, "x")
    partial = call(logits_kernel, (of_y * high * group, of_x * high * small), image, text)
    other = lax.ppermute(partial, "c", [(0, 1), (1, 0)])
    zl = lax.axis_index("zl")
    at = jnp.stack(
        [lax.axis_index("x"), lax.axis_index("y"), zl // near, lax.axis_index("zh") * near + zl % near]
    ).astype(jnp.int32)
    grad_i, grad_t = call(
        functools.partial(grads_kernel, (high, halves, small, rows, of_y)),
        [image.shape, text.shape],
        at, log_scale, logit_bias, partial, other, image, text,
        scalars=3,
    )
    back_i = exchange(grad_i, "y")
    back_t = exchange(grad_t, "x")
    sent = call(functools.partial(narrow_kernel, inner, narrow), (high * low, small, LANES), back_i, back_t)
    got = exchange(sent, ("zh", "zl"))
    out_i, out_t = call(functools.partial(collect_kernel, place), [(narrow, rows), (narrow, rows)], got)
    return (out_i.T, out_t.T)


def program(mesh, sizes):
    fine = Mesh(mesh.devices.reshape(sizes), ("x", "zh", "y", "zl", "c"))
    dp, mp = ("x", "zh", "y"), ("zl", "c")
    return jax.shard_map(
        on_device,
        mesh=fine,
        in_specs=(P(dp, mp), P(dp, mp), P(), P()),
        out_specs=(P(dp, mp), P(dp, mp)),
        check_vma=False,
    )


def solution(mesh):
    return program(mesh, (4, 2, 4, 16, 2))
```

```python
import functools

import jax
import jax.numpy as jnp
from jax import lax
from jax.experimental import pallas as pl
from jax.experimental.pallas import tpu as pltpu
from jax.sharding import Mesh, PartitionSpec as P

LANES = 128
SUB = 8
VMEM = pl.BlockSpec(memory_space=pltpu.VMEM)
SMEM = pl.BlockSpec(memory_space=pltpu.SMEM)


def rows_first(block):
    narrow, rows = block.shape
    filled = jnp.concatenate([block, jnp.zeros((LANES - narrow, rows), block.dtype)], axis=0)
    return filled.T


def shift(block, lanes):
    lanes = lanes % LANES
    return block if lanes == 0 else pltpu.roll(block, lanes, 1)


def take(tiles, at, width):
    tile, off = divmod(at, LANES)
    value = shift(tiles[tile], -off)
    lane = lax.broadcasted_iota(jnp.int32, value.shape, 1)
    if off + width > LANES:
        value = jnp.where(lane < LANES - off, value, shift(tiles[tile + 1], -off))
    return jnp.where(lane < width, value, 0.0)


def put(tiles, at, width, value):
    tile, off = divmod(at, LANES)
    moved = shift(value, off)
    pieces = [(tile, moved)]
    if off + width > LANES:
        lane = lax.broadcasted_iota(jnp.int32, value.shape, 1)
        pieces = [(tile, jnp.where(lane >= off, moved, 0.0)), (tile + 1, jnp.where(lane < off, moved, 0.0))]
    for which, part in pieces:
        tiles[which] = part if tiles[which] is None else tiles[which] + part


def load(ref, first, start, rows, width):
    found = []
    for lo in range(0, width, LANES):
        hi = min(lo + LANES, width)
        value = ref[first, start : start + rows, lo:hi]
        if hi - lo < LANES:
            value = jnp.concatenate([value, jnp.zeros((rows, LANES - hi + lo), value.dtype)], axis=1)
        found.append(value)
    return found


def store(ref, index, start, tiles, width):
    rows = tiles[0].shape[0]
    for tile, value in enumerate(tiles):
        lo = tile * LANES
        hi = min(lo + LANES, width)
        if index is None:
            ref[start : start + rows, lo:hi] = value[:, : hi - lo]
        else:
            ref[index, start : start + rows, lo:hi] = value[:, : hi - lo]


def tiles_of(lanes):
    return -(-lanes // LANES)


def filled(tiles):
    shape = next(t.shape for t in tiles if t is not None)
    return [jnp.zeros(shape, jnp.float32) if t is None else t for t in tiles]


def split_kernel(of_i, of_j, image_ref, text_ref, out_ref):
    narrow, rows = image_ref.shape
    image, text = rows_first(image_ref[...]), rows_first(text_ref[...])
    blocks_i, blocks_j = rows // of_i // SUB, rows // of_j // SUB
    width = out_ref.shape[2]

    def packed(block, first, count, lane_block):
        tiles = [None] * tiles_of(width)
        for k in range(count):
            start = (first + k) * SUB
            put(tiles, (lane_block + k) * narrow, narrow, block[start : start + SUB])
        return tiles

    images = [packed(image, i * blocks_i, blocks_i, 0) for i in range(of_i)]
    texts = [packed(text, j * blocks_j, blocks_j, blocks_i) for j in range(of_j)]
    for j in range(of_j):
        for i in range(of_i):
            tiles = [
                a if b is None else b if a is None else a + b for a, b in zip(images[i], texts[j])
            ]
            store(out_ref, j * of_i + i, 0, filled(tiles), width)


def widen_kernel(sizes, narrow, got_ref, image_ref, text_ref):
    of_i, of_j, blocks_i, blocks_j = sizes
    copies, _, wide = image_ref.shape
    rows = [[load(got_ref, j * of_i + i, 0, SUB, got_ref.shape[2]) for i in range(of_i)] for j in range(of_j)]
    for j in range(of_j):
        for k in range(blocks_i + blocks_j):
            tiles = [None] * tiles_of(wide)
            for i in range(of_i):
                put(tiles, i * narrow, narrow, take(rows[j][i], k * narrow, narrow))
            if k < blocks_i:
                for copy in range(copies):
                    store(image_ref, copy, (j * blocks_i + k) * SUB, tiles, wide)
            else:
                store(text_ref, None, (j * blocks_j + k - blocks_i) * SUB, tiles, wide)


def logits_kernel(image_ref, text_ref, out_ref):
    a, m, w = image_ref.shape
    out_ref[...] = lax.dot_general(
        image_ref[...].reshape(a * m, w),
        text_ref[...],
        (((1,), (1,)), ((), ())),
        preferred_element_type=jnp.float32,
        precision=lax.Precision.HIGHEST,
    )


def grads_kernel(sizes, at_ref, log_scale_ref, bias_ref, sums_ref, image_ref, text_ref, gi_ref, gt_ref):
    high, of_y, rows, group_i, group_j = sizes
    a, m, w = image_ref.shape
    scale = jnp.exp(jnp.full((1, 1), log_scale_ref[0], jnp.float32))
    logits = scale * (sums_ref[0] + sums_ref[1]) + bias_ref[0]
    x, y, i, j = at_ref[0], at_ref[1], at_ref[2], at_ref[3]
    r = lax.broadcasted_iota(jnp.int32, logits.shape, 0)
    source, zh, inner = r // m, (r % m) // group_i, r % group_i
    row_ids = ((source // of_y * high + zh) * of_y + source % of_y) * rows + i * group_i + inner
    c = lax.broadcasted_iota(jnp.int32, logits.shape, 1)
    zh, inner = c // group_j, c % group_j
    col_ids = ((x * high + zh) * of_y + y) * rows + j * group_j + inner
    label = jnp.where(row_ids == col_ids, 1.0, -1.0)
    coef = -label * jax.nn.sigmoid(-label * logits)
    dot = functools.partial(
        lax.dot_general, preferred_element_type=jnp.float32, precision=lax.Precision.HIGHEST
    )
    gi_ref[...] = (scale * dot(coef, text_ref[...], (((1,), (0,)), ((), ())))).reshape(a, m, w)
    gt_ref[...] = scale * dot(coef, image_ref[...].reshape(a * m, w), (((0,), (0,)), ((), ())))


def narrow_kernel(sizes, narrow, image_ref, text_ref, out_ref):
    of_i, of_j, blocks_i, blocks_j = sizes
    copies, _, wide = image_ref.shape
    width = out_ref.shape[2]
    for j in range(of_j):
        rows = []
        for k in range(blocks_i):
            start = (j * blocks_i + k) * SUB
            tiles = load(image_ref, 0, start, SUB, wide)
            for copy in range(1, copies):
                tiles = [a + b for a, b in zip(tiles, load(image_ref, copy, start, SUB, wide))]
            rows.append(tiles)
        for k in range(blocks_j):
            rows.append(load(text_ref, 0, (j * blocks_j + k) * SUB, SUB, wide))
        for i in range(of_i):
            tiles = [None] * tiles_of(width)
            for k, value in enumerate(rows):
                put(tiles, k * narrow, narrow, take(value, i * narrow, narrow))
            store(out_ref, j * of_i + i, 0, tiles, width)


def collect_kernel(sizes, got_ref, image_ref, text_ref):
    of_i, of_j, blocks_i, blocks_j = sizes
    narrow, rows = image_ref.shape
    width = got_ref.shape[2]

    def total(sources):
        tiles = load(got_ref, sources[0], 0, SUB, width)
        for source in sources[1:]:
            tiles = [a + b for a, b in zip(tiles, load(got_ref, source, 0, SUB, width))]
        return tiles

    images, texts = [], []
    for i in range(of_i):
        tiles = total([j * of_i + i for j in range(of_j)])
        images += [take(tiles, k * narrow, narrow) for k in range(blocks_i)]
    for j in range(of_j):
        tiles = total([j * of_i + i for i in range(of_i)])
        texts += [take(tiles, (blocks_i + k) * narrow, narrow) for k in range(blocks_j)]
    image_ref[...] = jnp.concatenate(images, axis=0).T[:narrow]
    text_ref[...] = jnp.concatenate(texts, axis=0).T[:narrow]


def call(kernel, outs, *operands, scalars=0):
    many = isinstance(outs, list)
    shapes = [jax.ShapeDtypeStruct(s, jnp.float32) for s in (outs if many else [outs])]
    return pl.pallas_call(
        kernel,
        out_shape=shapes if many else shapes[0],
        in_specs=[SMEM] * scalars + [VMEM] * (len(operands) - scalars),
        out_specs=[VMEM] * len(shapes) if many else VMEM,
        compiler_params=pltpu.CompilerParams(vmem_limit_bytes=32 * 1024 * 1024),
    )(*operands)


def exchange(value, axis):
    return lax.all_to_all(value, axis, split_axis=0, concat_axis=0, tiled=True)


def on_device(image_emb, text_emb, log_scale, logit_bias):
    of_x, of_j, of_y, of_i = (lax.axis_size(a) for a in ("x", "zh", "y", "zm"))
    rows, narrow = image_emb.shape
    group_i, group_j = rows // of_i, rows // of_j
    blocks = (of_i, of_j, group_i // SUB, group_j // SUB)
    wide = of_i * narrow
    packed = (of_j * of_i, SUB, tiles_of((group_i + group_j) // SUB * narrow) * LANES)

    sent = call(functools.partial(split_kernel, of_i, of_j), packed, image_emb.T, text_emb.T)
    got = exchange(sent, ("zh", "zm"))
    mine, text = call(
        functools.partial(widen_kernel, blocks, narrow),
        [(of_x * of_y, of_j * group_i, wide), (of_j * group_j, wide)],
        got,
    )
    image = exchange(mine, ("x", "y"))
    part = call(logits_kernel, (of_x * of_y * of_j * group_i, of_j * group_j), image, text)
    part = part + lax.ppermute(part, "ze", [(0, 1), (1, 0)])
    sums = lax.all_gather(part, "c")
    at = jnp.stack([lax.axis_index(a) for a in ("x", "y", "zm", "zh")]).astype(jnp.int32)
    grad_i, grad_t = call(
        functools.partial(grads_kernel, (of_j, of_y, rows, group_i, group_j)),
        [image.shape, text.shape],
        at, log_scale, logit_bias, sums, image, text,
        scalars=3,
    )
    back = exchange(grad_i, ("x", "y"))
    sent = call(functools.partial(narrow_kernel, blocks, narrow), packed, back, grad_t[None])
    got = exchange(sent, ("zh", "zm"))
    out_i, out_t = call(functools.partial(collect_kernel, blocks), [(narrow, rows), (narrow, rows)], got)
    return (out_i.T, out_t.T)


def program(mesh, sizes):
    x, zh, y, zl, c = sizes
    fine = Mesh(mesh.devices.reshape(x, zh, y, zl // 2, 2, c), ("x", "zh", "y", "zm", "ze", "c"))
    dp, mp = ("x", "zh", "y"), ("zm", "ze", "c")
    return jax.shard_map(
        on_device,
        mesh=fine,
        in_specs=(P(dp, mp), P(dp, mp), P(), P()),
        out_specs=(P(dp, mp), P(dp, mp)),
        check_vma=False,
    )


def solution(mesh):
    return program(mesh, (4, 2, 4, 16, 2))
```

```python
import functools

import jax
import jax.numpy as jnp
from jax import lax
from jax.experimental import pallas as pl
from jax.experimental.pallas import tpu as pltpu
from jax.sharding import Mesh, PartitionSpec as P

LANES = 128
SUB = 8
VMEM = pl.BlockSpec(memory_space=pltpu.VMEM)
SMEM = pl.BlockSpec(memory_space=pltpu.SMEM)


def rows_first(block):
    narrow, rows = block.shape
    filled = jnp.concatenate([block, jnp.zeros((LANES - narrow, rows), block.dtype)], axis=0)
    return filled.T


def shift(block, lanes):
    lanes = lanes % LANES
    return block if lanes == 0 else pltpu.roll(block, lanes, 1)


def tiles_of(lanes):
    return -(-lanes // LANES)


def lanes_from(off, shape):
    return lax.broadcasted_iota(jnp.int32, shape, 1) >= off


def pick(tile, at, width, to):
    which, off = divmod(at, LANES)
    value = tile(which)
    if off + width <= LANES:
        return shift(value, to - off)
    first, second = shift(value, -off), shift(tile(which + 1), -off)
    return shift(jnp.where(lanes_from(LANES - off, value.shape), second, first), to)


def packed(blocks, width):
    tiles = [None] * tiles_of(len(blocks) * width)
    for k, (tile, at) in enumerate(blocks):
        which, off = divmod(k * width, LANES)
        value = pick(tile, at, width, off)
        tiles[which] = value if tiles[which] is None else jnp.where(lanes_from(off, value.shape), value, tiles[which])
        if off + width > LANES:
            tiles[which + 1] = value
    return tiles


def reader(ref, first, start=0):
    def tile(which):
        lanes = slice(which * LANES, (which + 1) * LANES)
        if first is None:
            return ref[start : start + SUB, lanes]
        return ref[first, start : start + SUB, lanes]

    return tile


def split_kernel(of_i, of_j, image_any, text_any, out_ref, image_ref, text_ref, sems):
    copies = [
        pltpu.make_async_copy(image_any, image_ref, sems.at[0]),
        pltpu.make_async_copy(text_any, text_ref, sems.at[1]),
    ]
    for copy in copies:
        copy.start()
    for copy in copies:
        copy.wait()
    narrow, rows = image_ref.shape
    image, text = rows_first(image_ref[...]), rows_first(text_ref[...])
    blocks_i, blocks_j = rows // of_i // SUB, rows // of_j // SUB

    def block(rows_of, index):
        value = rows_of[index * SUB : (index + 1) * SUB]
        return (lambda which: value, 0)

    for j in range(of_j):
        texts = [block(text, j * blocks_j + k) for k in range(blocks_j)]
        for i in range(of_i):
            images = [block(image, i * blocks_i + k) for k in range(blocks_i)]
            for which, value in enumerate(packed(images + texts, narrow)):
                out_ref[j * of_i + i, :, which * LANES : (which + 1) * LANES] = value


def widen_kernel(sizes, narrow, got_ref, image_ref, text_ref):
    of_i, of_j, blocks_i, blocks_j = sizes
    copies = image_ref.shape[0]
    full, rest = divmod(of_i * narrow, LANES)
    last = None
    for j in range(of_j):
        sources = [reader(got_ref, j * of_i + i) for i in range(of_i)]
        for k in range(blocks_i + blocks_j):
            tiles = packed([(source, k * narrow) for source in sources], narrow)
            if k < blocks_i:
                group = j * blocks_i + k
                for copy in range(copies):
                    for which in range(full):
                        lo = (group * full + which) * LANES
                        image_ref[copy, :, lo : lo + LANES] = tiles[which]
                moved = shift(tiles[full], group * rest)
                last = moved if last is None else jnp.where(lanes_from(group * rest, moved.shape), moved, last)
            else:
                at = (j * blocks_j + k - blocks_i) * SUB
                tiles[full] = jnp.where(lanes_from(rest, tiles[full].shape), 0.0, tiles[full])
                for which, value in enumerate(tiles):
                    text_ref[at : at + SUB, which * LANES : (which + 1) * LANES] = value
    lo = of_j * blocks_i * full * LANES
    for copy in range(copies):
        image_ref[copy, :, lo : lo + LANES] = last


def stacked(image_ref, groups, full, rest):
    sources = image_ref.shape[0]
    lo = groups * full * LANES
    last = image_ref[:, :, lo : lo + LANES].reshape(sources * SUB, LANES)
    found = []
    for group in range(groups):
        at = group * full * LANES
        whole = image_ref[:, :, at : at + full * LANES].reshape(sources * SUB, full * LANES)
        found.append(jnp.concatenate([whole, shift(last, -group * rest)], axis=1))
    return jnp.concatenate(found, axis=0)


dot = functools.partial(
    lax.dot_general, preferred_element_type=jnp.float32, precision=lax.Precision.HIGHEST
)


def logits_kernel(tiling, image_ref, text_ref, out_ref):
    out_ref[...] = dot(stacked(image_ref, *tiling), text_ref[...], (((1,), (1,)), ((), ())))


def grads_kernel(sizes, tiling, at_ref, log_scale_ref, bias_ref, own_ref, far_ref, image_ref, text_ref, gi_ref, gt_ref):
    high, of_y, rows, group_i, group_j = sizes
    groups, full, rest = tiling
    sources = image_ref.shape[0]
    scale = jnp.exp(jnp.full((1, 1), log_scale_ref[0], jnp.float32))
    logits = scale * ((own_ref[0] + own_ref[1]) + (far_ref[0] + far_ref[1])) + bias_ref[0]
    x, y, i, j = at_ref[0], at_ref[1], at_ref[2], at_ref[3]
    r = lax.broadcasted_iota(jnp.int32, logits.shape, 0)
    group, source = r // (sources * SUB), r % (sources * SUB) // SUB
    blocks_i = group_i // SUB
    zh, inner = group // blocks_i, group % blocks_i * SUB + r % SUB
    row_ids = ((source // of_y * high + zh) * of_y + source % of_y) * rows + i * group_i + inner
    c = lax.broadcasted_iota(jnp.int32, logits.shape, 1)
    zh, inner = c // group_j, c % group_j
    col_ids = ((x * high + zh) * of_y + y) * rows + j * group_j + inner
    label = jnp.where(row_ids == col_ids, 1.0, -1.0)
    coef = -label * jax.nn.sigmoid(-label * logits)
    found = scale * dot(coef, text_ref[...], (((1,), (0,)), ((), ())))
    last = None
    for group in range(groups):
        part = found[group * sources * SUB : (group + 1) * sources * SUB]
        at = group * full * LANES
        gi_ref[:, :, at : at + full * LANES] = part[:, : full * LANES].reshape(sources, SUB, full * LANES)
        moved = shift(part[:, full * LANES :], group * rest)
        last = moved if last is None else last + moved
    lo = groups * full * LANES
    gi_ref[:, :, lo : lo + LANES] = last.reshape(sources, SUB, LANES)
    gt_ref[...] = scale * dot(coef, stacked(image_ref, *tiling), (((0,), (0,)), ((), ())))


def narrow_kernel(sizes, narrow, image_ref, text_ref, out_ref):
    of_i, of_j, blocks_i, blocks_j = sizes
    full, rest = divmod(of_i * narrow, LANES)
    total = image_ref[0]
    for copy in range(1, image_ref.shape[0]):
        total = total + image_ref[copy]
    lo = of_j * blocks_i * full
    tiles = [total[:, k * LANES : (k + 1) * LANES] for k in range(lo + 1)]

    def image_row(group):
        row = tiles[group * full : (group + 1) * full] + [shift(tiles[lo], -group * rest)]
        return lambda which: row[which]

    for j in range(of_j):
        rows = [image_row(j * blocks_i + k) for k in range(blocks_i)]
        rows += [reader(text_ref, None, (j * blocks_j + k) * SUB) for k in range(blocks_j)]
        for i in range(of_i):
            for which, value in enumerate(packed([(row, i * narrow) for row in rows], narrow)):
                out_ref[j * of_i + i, :, which * LANES : (which + 1) * LANES] = value


def collect_kernel(sizes, got_ref, image_ref, text_ref):
    of_i, of_j, blocks_i, blocks_j = sizes
    narrow = image_ref.shape[0]

    def total(sources, first, last):
        tiles = {}
        for which in range(first * narrow // LANES, tiles_of(last * narrow)):
            tiles[which] = reader(got_ref, sources[0])(which)
            for source in sources[1:]:
                tiles[which] = tiles[which] + reader(got_ref, source)(which)
        return [pick(lambda which: tiles[which], k * narrow, narrow, 0) for k in range(first, last)]

    images, texts = [], []
    for i in range(of_i):
        images += total([j * of_i + i for j in range(of_j)], 0, blocks_i)
    for j in range(of_j):
        texts += total([j * of_i + i for i in range(of_i)], blocks_i, blocks_i + blocks_j)
    image_ref[...] = jnp.concatenate(images, axis=0).T[:narrow]
    text_ref[...] = jnp.concatenate(texts, axis=0).T[:narrow]


def call(kernel, outs, *operands, scalars=0, inputs=VMEM, scratch=()):
    many = isinstance(outs, list)
    shapes = [jax.ShapeDtypeStruct(s, jnp.float32) for s in (outs if many else [outs])]
    return pl.pallas_call(
        kernel,
        out_shape=shapes if many else shapes[0],
        in_specs=[SMEM] * scalars + [inputs] * (len(operands) - scalars),
        out_specs=[VMEM] * len(shapes) if many else VMEM,
        scratch_shapes=list(scratch),
        compiler_params=pltpu.CompilerParams(vmem_limit_bytes=32 * 1024 * 1024),
    )(*operands)


def exchange(value, axis):
    return lax.all_to_all(value, axis, split_axis=0, concat_axis=0, tiled=True)


def on_device(image_emb, text_emb, log_scale, logit_bias):
    of_x, of_j, of_y, of_i = (lax.axis_size(a) for a in ("x", "zh", "y", "zm"))
    rows, narrow = image_emb.shape
    group_i, group_j = rows // of_i, rows // of_j
    blocks = (of_i, of_j, group_i // SUB, group_j // SUB)
    full, rest = divmod(of_i * narrow, LANES)
    groups = of_j * blocks[2]
    assert 0 < rest * groups <= LANES
    tiling = (groups, full, rest)
    plane = of_x * of_y
    sent_shape = (of_j * of_i, SUB, tiles_of((blocks[2] + blocks[3]) * narrow) * LANES)
    block = pltpu.VMEM((narrow, rows), jnp.float32)

    sent = call(
        functools.partial(split_kernel, of_i, of_j), sent_shape, image_emb.T, text_emb.T,
        inputs=pl.BlockSpec(memory_space=pl.ANY), scratch=[block, block, pltpu.SemaphoreType.DMA((2,))],
    )
    got = exchange(sent, ("zh", "zm"))
    mine, text = call(
        functools.partial(widen_kernel, blocks, narrow),
        [(plane, SUB, (groups * full + 1) * LANES), (of_j * group_j, (full + 1) * LANES)],
        got,
    )
    image = exchange(mine, ("x", "y"))
    part = call(functools.partial(logits_kernel, tiling), (plane * groups * SUB, of_j * group_j), image, text)
    other = lax.ppermute(part, "ze", [(0, 1), (1, 0)])
    own = lax.all_gather(part, "c")
    far = lax.all_gather(other, "c")
    at = jnp.stack([lax.axis_index(a) for a in ("x", "y", "zm", "zh")]).astype(jnp.int32)
    grad_i, grad_t = call(
        functools.partial(grads_kernel, (of_j, of_y, rows, group_i, group_j), tiling),
        [image.shape, text.shape],
        at, log_scale, logit_bias, own, far, image, text,
        scalars=3,
    )
    back = exchange(grad_i, ("x", "y"))
    sent = call(functools.partial(narrow_kernel, blocks, narrow), sent_shape, back, grad_t)
    got = exchange(sent, ("zh", "zm"))
    out_i, out_t = call(functools.partial(collect_kernel, blocks), [(narrow, rows), (narrow, rows)], got)
    return (out_i.T, out_t.T)


def program(mesh, sizes):
    x, zh, y, zl, c = sizes
    fine = Mesh(mesh.devices.reshape(x, zh, y, zl // 2, 2, c), ("x", "zh", "y", "zm", "ze", "c"))
    dp, mp = ("x", "zh", "y"), ("zm", "ze", "c")
    return jax.shard_map(
        on_device,
        mesh=fine,
        in_specs=(P(dp, mp), P(dp, mp), P(), P()),
        out_specs=(P(dp, mp), P(dp, mp)),
        check_vma=False,
    )


def solution(mesh):
    return program(mesh, (4, 2, 4, 16, 2))
```

```python
import functools

import jax
import jax.numpy as jnp
from jax import lax
from jax.experimental import pallas as pl
from jax.experimental.pallas import tpu as pltpu
from jax.sharding import Mesh, PartitionSpec as P

LANES = 128
SUB = 8
VMEM = pl.BlockSpec(memory_space=pltpu.VMEM)
SMEM = pl.BlockSpec(memory_space=pltpu.SMEM)


def rows_first(block):
    narrow, rows = block.shape
    filled = jnp.concatenate([block, jnp.zeros((LANES - narrow, rows), block.dtype)], axis=0)
    return filled.T


def shift(block, lanes):
    lanes = lanes % LANES
    return block if lanes == 0 else pltpu.roll(block, lanes, 1)


def tiles_of(lanes):
    return -(-lanes // LANES)


def lanes_from(off, shape):
    return lax.broadcasted_iota(jnp.int32, shape, 1) >= off


def pick(tile, at, width, to):
    which, off = divmod(at, LANES)
    value = tile(which)
    if off + width <= LANES:
        return shift(value, to - off)
    first, second = shift(value, -off), shift(tile(which + 1), -off)
    return shift(jnp.where(lanes_from(LANES - off, value.shape), second, first), to)


def packed(blocks, width):
    tiles = [None] * tiles_of(len(blocks) * width)
    for k, (tile, at) in enumerate(blocks):
        which, off = divmod(k * width, LANES)
        value = pick(tile, at, width, off)
        tiles[which] = value if tiles[which] is None else jnp.where(lanes_from(off, value.shape), value, tiles[which])
        if off + width > LANES:
            tiles[which + 1] = value
    return tiles


def reader(ref, first, start=0):
    def tile(which):
        lanes = slice(which * LANES, (which + 1) * LANES)
        if first is None:
            return ref[start : start + SUB, lanes]
        return ref[first, start : start + SUB, lanes]

    return tile


def split_kernel(of_i, of_j, image_hbm, text_hbm, out_ref, image_ref, text_ref, sems):
    copies = [
        pltpu.make_async_copy(image_hbm, image_ref, sems.at[0]),
        pltpu.make_async_copy(text_hbm, text_ref, sems.at[1]),
    ]
    for copy in copies:
        copy.start()
    for copy in copies:
        copy.wait()
    narrow, rows = image_ref.shape
    image, text = rows_first(image_ref[...]), rows_first(text_ref[...])
    blocks_i, blocks_j = rows // of_i // SUB, rows // of_j // SUB

    def block(rows_of, index):
        value = rows_of[index * SUB : (index + 1) * SUB]
        return (lambda which: value, 0)

    for j in range(of_j):
        texts = [block(text, j * blocks_j + k) for k in range(blocks_j)]
        for i in range(of_i):
            images = [block(image, i * blocks_i + k) for k in range(blocks_i)]
            for which, value in enumerate(packed(images + texts, narrow)):
                out_ref[j * of_i + i, :, which * LANES : (which + 1) * LANES] = value


def widen_kernel(sizes, narrow, got_ref, image_ref, text_ref):
    of_i, of_j, blocks_i, blocks_j = sizes
    copies = image_ref.shape[0]
    full, rest = divmod(of_i * narrow, LANES)
    last = None
    for j in range(of_j):
        sources = [reader(got_ref, j * of_i + i) for i in range(of_i)]
        for k in range(blocks_i + blocks_j):
            tiles = packed([(source, k * narrow) for source in sources], narrow)
            if k < blocks_i:
                group = j * blocks_i + k
                for copy in range(copies):
                    for which in range(full):
                        lo = (group * full + which) * LANES
                        image_ref[copy, :, lo : lo + LANES] = tiles[which]
                moved = shift(tiles[full], group * rest)
                last = moved if last is None else jnp.where(lanes_from(group * rest, moved.shape), moved, last)
            else:
                at = (j * blocks_j + k - blocks_i) * SUB
                tiles[full] = jnp.where(lanes_from(rest, tiles[full].shape), 0.0, tiles[full])
                for which, value in enumerate(tiles):
                    text_ref[at : at + SUB, which * LANES : (which + 1) * LANES] = value
    lo = of_j * blocks_i * full * LANES
    for copy in range(copies):
        image_ref[copy, :, lo : lo + LANES] = last


def stacked(image_ref, groups, full, rest):
    sources = image_ref.shape[0]
    lo = groups * full * LANES
    last = image_ref[:, :, lo : lo + LANES].reshape(sources * SUB, LANES)
    found = []
    for group in range(groups):
        at = group * full * LANES
        whole = image_ref[:, :, at : at + full * LANES].reshape(sources * SUB, full * LANES)
        found.append(jnp.concatenate([whole, shift(last, -group * rest)], axis=1))
    return jnp.concatenate(found, axis=0)


dot = functools.partial(
    lax.dot_general, preferred_element_type=jnp.float32, precision=lax.Precision.HIGHEST
)


def logits_kernel(tiling, image_ref, text_ref, out_ref):
    out_ref[...] = dot(stacked(image_ref, *tiling), text_ref[...], (((1,), (1,)), ((), ())))


def grads_kernel(sizes, tiling, log_scale_ref, bias_ref, both_ref, image_ref, text_ref, gi_ref, gt_ref):
    high, of_y, rows, group_i, group_j = sizes
    groups, full, rest = tiling
    sources = image_ref.shape[0]
    scale = jnp.exp(jnp.full((1, 1), log_scale_ref[0], jnp.float32))
    logits = scale * (both_ref[0] + both_ref[1]) + bias_ref[0]
    x, y, i, j = (lax.axis_index(a) for a in ("x", "y", "zm", "zh"))
    r = lax.broadcasted_iota(jnp.int32, logits.shape, 0)
    group, source = r // (sources * SUB), r % (sources * SUB) // SUB
    blocks_i = group_i // SUB
    zh, inner = group // blocks_i, group % blocks_i * SUB + r % SUB
    row_ids = ((source // of_y * high + zh) * of_y + source % of_y) * rows + i * group_i + inner
    c = lax.broadcasted_iota(jnp.int32, logits.shape, 1)
    zh, inner = c // group_j, c % group_j
    col_ids = ((x * high + zh) * of_y + y) * rows + j * group_j + inner
    label = jnp.where(row_ids == col_ids, 1.0, -1.0)
    coef = -label * jax.nn.sigmoid(-label * logits)
    coef = scale * coef
    found = dot(coef, text_ref[...], (((1,), (0,)), ((), ())))
    last = None
    for group in range(groups):
        part = found[group * sources * SUB : (group + 1) * sources * SUB]
        at = group * full * LANES
        gi_ref[:, :, at : at + full * LANES] = part[:, : full * LANES].reshape(sources, SUB, full * LANES)
        moved = shift(part[:, full * LANES :], group * rest)
        last = moved if last is None else last + moved
    lo = groups * full * LANES
    gi_ref[:, :, lo : lo + LANES] = last.reshape(sources, SUB, LANES)
    gt_ref[...] = dot(coef, stacked(image_ref, *tiling), (((0,), (0,)), ((), ())))


def narrow_kernel(sizes, narrow, image_ref, text_ref, out_ref):
    of_i, of_j, blocks_i, blocks_j = sizes
    full, rest = divmod(of_i * narrow, LANES)
    total = image_ref[0]
    for copy in range(1, image_ref.shape[0]):
        total = total + image_ref[copy]
    lo = of_j * blocks_i * full
    tiles = [total[:, k * LANES : (k + 1) * LANES] for k in range(lo + 1)]

    def image_row(group):
        row = tiles[group * full : (group + 1) * full] + [shift(tiles[lo], -group * rest)]
        return lambda which: row[which]

    for j in range(of_j):
        rows = [image_row(j * blocks_i + k) for k in range(blocks_i)]
        rows += [reader(text_ref, None, (j * blocks_j + k) * SUB) for k in range(blocks_j)]
        for i in range(of_i):
            for which, value in enumerate(packed([(row, i * narrow) for row in rows], narrow)):
                out_ref[j * of_i + i, :, which * LANES : (which + 1) * LANES] = value


def collect_kernel(sizes, got_ref, image_ref, text_ref):
    of_i, of_j, blocks_i, blocks_j = sizes
    narrow = image_ref.shape[0]

    def total(sources, first, last):
        tiles = {}
        for which in range(first * narrow // LANES, tiles_of(last * narrow)):
            tiles[which] = reader(got_ref, sources[0])(which)
            for source in sources[1:]:
                tiles[which] = tiles[which] + reader(got_ref, source)(which)
        return [pick(lambda which: tiles[which], k * narrow, narrow, 0) for k in range(first, last)]

    images, texts = [], []
    for i in range(of_i):
        images += total([j * of_i + i for j in range(of_j)], 0, blocks_i)
    for j in range(of_j):
        texts += total([j * of_i + i for i in range(of_i)], blocks_i, blocks_i + blocks_j)
    image_ref[...] = jnp.concatenate(images, axis=0).T[:narrow]
    text_ref[...] = jnp.concatenate(texts, axis=0).T[:narrow]


def call(kernel, outs, *operands, inputs=None, scratch=()):
    many = isinstance(outs, list)
    shapes = [jax.ShapeDtypeStruct(s, jnp.float32) for s in (outs if many else [outs])]
    return pl.pallas_call(
        kernel,
        out_shape=shapes if many else shapes[0],
        in_specs=inputs or [VMEM] * len(operands),
        out_specs=[VMEM] * len(shapes) if many else VMEM,
        scratch_shapes=list(scratch),
        compiler_params=pltpu.CompilerParams(vmem_limit_bytes=32 * 1024 * 1024),
    )(*operands)


def exchange(value, axis):
    return lax.all_to_all(value, axis, split_axis=0, concat_axis=0, tiled=True)


def on_device(image_emb, text_emb, log_scale, logit_bias):
    of_x, of_j, of_y, of_i = (lax.axis_size(a) for a in ("x", "zh", "y", "zm"))
    rows, narrow = image_emb.shape
    group_i, group_j = rows // of_i, rows // of_j
    blocks = (of_i, of_j, group_i // SUB, group_j // SUB)
    full, rest = divmod(of_i * narrow, LANES)
    groups = of_j * blocks[2]
    assert 0 < rest * groups <= LANES
    tiling = (groups, full, rest)
    plane = of_x * of_y
    sent_shape = (of_j * of_i, SUB, tiles_of((blocks[2] + blocks[3]) * narrow) * LANES)
    block = pltpu.VMEM((narrow, rows), jnp.float32)

    held = [pltpu.with_memory_space_constraint(a.T, pltpu.HBM) for a in (image_emb, text_emb)]
    sent = call(
        functools.partial(split_kernel, of_i, of_j), sent_shape, *held,
        inputs=[pl.BlockSpec(memory_space=pltpu.HBM)] * 2,
        scratch=[block, block, pltpu.SemaphoreType.DMA((2,))],
    )
    got = exchange(sent, ("zh", "zm"))
    mine, text = call(
        functools.partial(widen_kernel, blocks, narrow),
        [(plane, SUB, (groups * full + 1) * LANES), (of_j * group_j, (full + 1) * LANES)],
        got,
    )
    image = exchange(mine, ("x", "y"))
    part = call(functools.partial(logits_kernel, tiling), (plane * groups * SUB, of_j * group_j), image, text)
    other = lax.ppermute(part, "ze", [(0, 1), (1, 0)])
    both = lax.all_gather(part + other, "c")
    grad_i, grad_t = call(
        functools.partial(grads_kernel, (of_j, of_y, rows, group_i, group_j), tiling),
        [image.shape, text.shape],
        log_scale, logit_bias, both, image, text,
        inputs=[SMEM] * 2 + [VMEM] * 3,
    )
    back = exchange(grad_i, ("x", "y"))
    sent = call(functools.partial(narrow_kernel, blocks, narrow), sent_shape, back, grad_t)
    got = exchange(sent, ("zh", "zm"))
    out_i, out_t = call(functools.partial(collect_kernel, blocks), [(narrow, rows), (narrow, rows)], got)
    return (out_i.T, out_t.T)


def program(mesh, sizes):
    x, zh, y, zl, c = sizes
    fine = Mesh(mesh.devices.reshape(x, zh, y, zl // 2, 2, c), ("x", "zh", "y", "zm", "ze", "c"))
    dp, mp = ("x", "zh", "y"), ("zm", "ze", "c")
    return jax.shard_map(
        on_device,
        mesh=fine,
        in_specs=(P(dp, mp), P(dp, mp), P(), P()),
        out_specs=(P(dp, mp), P(dp, mp)),
        check_vma=False,
    )


def solution(mesh):
    return program(mesh, (4, 2, 4, 16, 2))
```

```python
import functools

import jax
import jax.numpy as jnp
from jax import lax
from jax.experimental import pallas as pl
from jax.experimental.pallas import tpu as pltpu
from jax.sharding import Mesh, PartitionSpec as P

LANES = 128
SUB = 8
VMEM = pl.BlockSpec(memory_space=pltpu.VMEM)
SMEM = pl.BlockSpec(memory_space=pltpu.SMEM)


def rows_first(block):
    narrow, rows = block.shape
    filled = jnp.concatenate([block, jnp.zeros((LANES - narrow, rows), block.dtype)], axis=0)
    return filled.T


def shift(block, lanes):
    lanes = lanes % LANES
    return block if lanes == 0 else pltpu.roll(block, lanes, 1)


def tiles_of(lanes):
    return -(-lanes // LANES)


def lanes_from(off, shape):
    return lax.broadcasted_iota(jnp.int32, shape, 1) >= off


def pick(tile, at, width, to):
    which, off = divmod(at, LANES)
    value = tile(which)
    if off + width <= LANES:
        return shift(value, to - off)
    first, second = shift(value, -off), shift(tile(which + 1), -off)
    return shift(jnp.where(lanes_from(LANES - off, value.shape), second, first), to)


def packed(blocks, width):
    tiles = [None] * tiles_of(len(blocks) * width)
    for k, (tile, at) in enumerate(blocks):
        which, off = divmod(k * width, LANES)
        value = pick(tile, at, width, off)
        tiles[which] = value if tiles[which] is None else jnp.where(lanes_from(off, value.shape), value, tiles[which])
        if off + width > LANES:
            tiles[which + 1] = value
    return tiles


def reader(ref, first, start=0):
    def tile(which):
        lanes = slice(which * LANES, (which + 1) * LANES)
        if first is None:
            return ref[start : start + SUB, lanes]
        return ref[first, start : start + SUB, lanes]

    return tile


def split_kernel(of_i, of_j, image_hbm, text_hbm, out_ref, image_ref, text_ref, sems):
    copies = [
        pltpu.make_async_copy(image_hbm, image_ref, sems.at[0]),
        pltpu.make_async_copy(text_hbm, text_ref, sems.at[1]),
    ]
    for copy in copies:
        copy.start()
    for copy in copies:
        copy.wait()
    narrow, rows = image_ref.shape
    image, text = rows_first(image_ref[...]), rows_first(text_ref[...])
    blocks_i, blocks_j = rows // of_i // SUB, rows // of_j // 2 // SUB

    def block(rows_of, index):
        value = rows_of[index * SUB : (index + 1) * SUB]
        return (lambda which: value, 0)

    for j in range(of_j):
        for i in range(of_i):
            texts = [block(text, (j * 2 + i % 2) * blocks_j + k) for k in range(blocks_j)]
            images = [block(image, i * blocks_i + k) for k in range(blocks_i)]
            for which, value in enumerate(packed(images + texts, narrow)):
                out_ref[j * of_i + i, :, which * LANES : (which + 1) * LANES] = value


def widen_kernel(sizes, narrow, got_ref, image_ref, text_ref):
    of_i, of_j, blocks_i, blocks_j = sizes
    copies = image_ref.shape[0]
    full, rest = divmod(of_i * narrow, LANES)
    last = None
    for j in range(of_j):
        sources = [reader(got_ref, j * of_i + i) for i in range(of_i)]
        for k in range(blocks_i + blocks_j):
            tiles = packed([(source, k * narrow) for source in sources], narrow)
            if k < blocks_i:
                group = j * blocks_i + k
                for copy in range(copies):
                    for which in range(full):
                        lo = (group * full + which) * LANES
                        image_ref[copy, :, lo : lo + LANES] = tiles[which]
                moved = shift(tiles[full], group * rest)
                last = moved if last is None else jnp.where(lanes_from(group * rest, moved.shape), moved, last)
            else:
                at = (j * blocks_j + k - blocks_i) * SUB
                tiles[full] = jnp.where(lanes_from(rest, tiles[full].shape), 0.0, tiles[full])
                for which, value in enumerate(tiles):
                    text_ref[at : at + SUB, which * LANES : (which + 1) * LANES] = value
    lo = of_j * blocks_i * full * LANES
    for copy in range(copies):
        image_ref[copy, :, lo : lo + LANES] = last


def stacked(image_ref, groups, full, rest):
    sources = image_ref.shape[0]
    lo = groups * full * LANES
    last = image_ref[:, :, lo : lo + LANES].reshape(sources * SUB, LANES)
    found = []
    for group in range(groups):
        at = group * full * LANES
        whole = image_ref[:, :, at : at + full * LANES].reshape(sources * SUB, full * LANES)
        found.append(jnp.concatenate([whole, shift(last, -group * rest)], axis=1))
    return jnp.concatenate(found, axis=0)


dot = functools.partial(
    lax.dot_general, preferred_element_type=jnp.float32, precision=lax.Precision.HIGHEST
)


def both_halves(text_ref, pair_ref):
    return jnp.concatenate([text_ref[...], pair_ref[...]], axis=0)


def logits_kernel(tiling, image_ref, text_ref, pair_ref, out_ref):
    text = both_halves(text_ref, pair_ref)
    out_ref[...] = dot(stacked(image_ref, *tiling), text, (((1,), (1,)), ((), ())))


def grads_kernel(sizes, tiling, log_scale_ref, bias_ref, both_ref, *refs):
    image_ref, text_ref, pair_ref, gi_ref, gt_ref, gt_pair_ref = refs
    high, of_y, rows, group_i, group_j = sizes
    groups, full, rest = tiling
    sources = image_ref.shape[0]
    scale = jnp.exp(jnp.full((1, 1), log_scale_ref[0], jnp.float32))
    logits = scale * (both_ref[0] + both_ref[1]) + bias_ref[0]
    x, y, i, j = (lax.axis_index(a) for a in ("x", "y", "zm", "zh"))
    r = lax.broadcasted_iota(jnp.int32, logits.shape, 0)
    group, source = r // (sources * SUB), r % (sources * SUB) // SUB
    blocks_i = group_i // SUB
    zh, inner = group // blocks_i, group % blocks_i * SUB + r % SUB
    row_ids = ((source // of_y * high + zh) * of_y + source % of_y) * rows + i * group_i + inner
    c = lax.broadcasted_iota(jnp.int32, logits.shape, 1)
    half, of_half = group_j // 2, text_ref.shape[0]
    which = (i + c // of_half) % 2
    zh, inner = c % of_half // half, c % half
    col_ids = ((x * high + zh) * of_y + y) * rows + j * group_j + which * half + inner
    label = jnp.where(row_ids == col_ids, 1.0, -1.0)
    coef = -label * jax.nn.sigmoid(-label * logits)
    coef = scale * coef
    found = dot(coef, both_halves(text_ref, pair_ref), (((1,), (0,)), ((), ())))
    last = None
    for group in range(groups):
        part = found[group * sources * SUB : (group + 1) * sources * SUB]
        at = group * full * LANES
        gi_ref[:, :, at : at + full * LANES] = part[:, : full * LANES].reshape(sources, SUB, full * LANES)
        moved = shift(part[:, full * LANES :], group * rest)
        last = moved if last is None else last + moved
    lo = groups * full * LANES
    gi_ref[:, :, lo : lo + LANES] = last.reshape(sources, SUB, LANES)
    found = dot(coef, stacked(image_ref, *tiling), (((0,), (0,)), ((), ())))
    gt_ref[...] = found[:of_half]
    gt_pair_ref[...] = found[of_half:]


def narrow_kernel(sizes, narrow, image_ref, text_ref, pair_ref, out_ref):
    of_i, of_j, blocks_i, blocks_j = sizes
    full, rest = divmod(of_i * narrow, LANES)
    total = image_ref[0]
    for copy in range(1, image_ref.shape[0]):
        total = total + image_ref[copy]
    lo = of_j * blocks_i * full
    tiles = [total[:, k * LANES : (k + 1) * LANES] for k in range(lo + 1)]

    def image_row(group):
        row = tiles[group * full : (group + 1) * full] + [shift(tiles[lo], -group * rest)]
        return lambda which: row[which]

    def text_row(start):
        own, pair = reader(text_ref, None, start), reader(pair_ref, None, start)
        row = [own(which) + pair(which) for which in range(full + 1)]
        return lambda which: row[which]

    for j in range(of_j):
        rows = [image_row(j * blocks_i + k) for k in range(blocks_i)]
        rows += [text_row((j * blocks_j + k) * SUB) for k in range(blocks_j)]
        for i in range(of_i):
            for which, value in enumerate(packed([(row, i * narrow) for row in rows], narrow)):
                out_ref[j * of_i + i, :, which * LANES : (which + 1) * LANES] = value


def collect_kernel(sizes, got_ref, image_ref, text_ref):
    of_i, of_j, blocks_i, blocks_j = sizes
    narrow = image_ref.shape[0]

    def total(sources, first, last):
        tiles = {}
        for which in range(first * narrow // LANES, tiles_of(last * narrow)):
            tiles[which] = reader(got_ref, sources[0])(which)
            for source in sources[1:]:
                tiles[which] = tiles[which] + reader(got_ref, source)(which)
        return [pick(lambda which: tiles[which], k * narrow, narrow, 0) for k in range(first, last)]

    images, texts = [], []
    for i in range(of_i):
        images += total([j * of_i + i for j in range(of_j)], 0, blocks_i)
    for j in range(of_j):
        for half in range(2):
            texts += total([j * of_i + i for i in range(half, of_i, 2)], blocks_i, blocks_i + blocks_j)
    image_ref[...] = jnp.concatenate(images, axis=0).T[:narrow]
    text_ref[...] = jnp.concatenate(texts, axis=0).T[:narrow]


def call(kernel, outs, *operands, inputs=None, scratch=()):
    many = isinstance(outs, list)
    shapes = [jax.ShapeDtypeStruct(s, jnp.float32) for s in (outs if many else [outs])]
    return pl.pallas_call(
        kernel,
        out_shape=shapes if many else shapes[0],
        in_specs=inputs or [VMEM] * len(operands),
        out_specs=[VMEM] * len(shapes) if many else VMEM,
        scratch_shapes=list(scratch),
        compiler_params=pltpu.CompilerParams(vmem_limit_bytes=32 * 1024 * 1024),
    )(*operands)


def exchange(value, axis):
    return lax.all_to_all(value, axis, split_axis=0, concat_axis=0, tiled=True)


def on_device(image_emb, text_emb, log_scale, logit_bias):
    of_x, of_j, of_y, of_i = (lax.axis_size(a) for a in ("x", "zh", "y", "zm"))
    rows, narrow = image_emb.shape
    group_i, group_j = rows // of_i, rows // of_j
    blocks = (of_i, of_j, group_i // SUB, group_j // 2 // SUB)
    full, rest = divmod(of_i * narrow, LANES)
    groups = of_j * blocks[2]
    assert 0 < rest * groups <= LANES
    tiling = (groups, full, rest)
    plane = of_x * of_y
    sent_shape = (of_j * of_i, SUB, tiles_of((blocks[2] + blocks[3]) * narrow) * LANES)
    block = pltpu.VMEM((narrow, rows), jnp.float32)

    held = [pltpu.with_memory_space_constraint(a.T, pltpu.HBM) for a in (image_emb, text_emb)]
    sent = call(
        functools.partial(split_kernel, of_i, of_j), sent_shape, *held,
        inputs=[pl.BlockSpec(memory_space=pltpu.HBM)] * 2,
        scratch=[block, block, pltpu.SemaphoreType.DMA((2,))],
    )
    got = exchange(sent, ("zh", "zm"))
    mine, text = call(
        functools.partial(widen_kernel, blocks, narrow),
        [(plane, SUB, (groups * full + 1) * LANES), (of_j * group_j // 2, (full + 1) * LANES)],
        got,
    )
    pairs = [(k, k ^ 1) for k in range(of_i)]
    pair = lax.ppermute(text, "zm", pairs)
    image = exchange(mine, ("x", "y"))
    part = call(functools.partial(logits_kernel, tiling), (plane * groups * SUB, of_j * group_j), image, text, pair)
    other = lax.ppermute(part, "ze", [(0, 1), (1, 0)])
    both = lax.all_gather(part + other, "c")
    grad_i, grad_t, grad_pair = call(
        functools.partial(grads_kernel, (of_j, of_y, rows, group_i, group_j), tiling),
        [image.shape, text.shape, text.shape],
        log_scale, logit_bias, both, image, text, pair,
        inputs=[SMEM] * 2 + [VMEM] * 4,
    )
    back_t = lax.ppermute(grad_pair, "zm", pairs)
    back = exchange(grad_i, ("x", "y"))
    sent = call(functools.partial(narrow_kernel, blocks, narrow), sent_shape, back, grad_t, back_t)
    got = exchange(sent, ("zh", "zm"))
    out_i, out_t = call(functools.partial(collect_kernel, blocks), [(narrow, rows), (narrow, rows)], got)
    return (out_i.T, out_t.T)


def program(mesh, sizes):
    x, zh, y, zl, c = sizes
    fine = Mesh(mesh.devices.reshape(x, zh, y, zl // 2, 2, c), ("x", "zh", "y", "zm", "ze", "c"))
    dp, mp = ("x", "zh", "y"), ("zm", "ze", "c")
    return jax.shard_map(
        on_device,
        mesh=fine,
        in_specs=(P(dp, mp), P(dp, mp), P(), P()),
        out_specs=(P(dp, mp), P(dp, mp)),
        check_vma=False,
    )


def solution(mesh):
    return program(mesh, (4, 2, 4, 16, 2))
```

```python
import functools

import jax
import jax.numpy as jnp
from jax import lax
from jax.experimental import pallas as pl
from jax.experimental.pallas import tpu as pltpu
from jax.sharding import Mesh, PartitionSpec as P

LANES = 128
SUB = 8
VMEM = pl.BlockSpec(memory_space=pltpu.VMEM)
SMEM = pl.BlockSpec(memory_space=pltpu.SMEM)


def rows_first(block):
    narrow, rows = block.shape
    filled = jnp.concatenate([block, jnp.zeros((LANES - narrow, rows), block.dtype)], axis=0)
    return filled.T


def shift(block, lanes):
    lanes = lanes % LANES
    return block if lanes == 0 else pltpu.roll(block, lanes, 1)


def tiles_of(lanes):
    return -(-lanes // LANES)


def lanes_from(off, shape):
    return lax.broadcasted_iota(jnp.int32, shape, 1) >= off


def pick(tile, at, width, to):
    which, off = divmod(at, LANES)
    value = tile(which)
    if off + width <= LANES:
        return shift(value, to - off)
    first, second = shift(value, -off), shift(tile(which + 1), -off)
    return shift(jnp.where(lanes_from(LANES - off, value.shape), second, first), to)


def packed(blocks, width):
    tiles = [None] * tiles_of(len(blocks) * width)
    for k, (tile, at) in enumerate(blocks):
        which, off = divmod(k * width, LANES)
        value = pick(tile, at, width, off)
        tiles[which] = value if tiles[which] is None else jnp.where(lanes_from(off, value.shape), value, tiles[which])
        if off + width > LANES:
            tiles[which + 1] = value
    return tiles


def reader(ref, first, start=0):
    def tile(which):
        lanes = slice(which * LANES, (which + 1) * LANES)
        if first is None:
            return ref[start : start + SUB, lanes]
        return ref[first, start : start + SUB, lanes]

    return tile


def split_kernel(of_i, of_j, image_hbm, text_hbm, out_ref, image_ref, text_ref, sems):
    copies = [
        pltpu.make_async_copy(image_hbm, image_ref, sems.at[0]),
        pltpu.make_async_copy(text_hbm, text_ref, sems.at[1]),
    ]
    for copy in copies:
        copy.start()
    for copy in copies:
        copy.wait()
    narrow, rows = image_ref.shape
    image, text = rows_first(image_ref[...]), rows_first(text_ref[...])
    blocks_i, blocks_j = rows // of_i // SUB, rows // of_j // 2 // SUB

    def block(rows_of, index):
        value = rows_of[index * SUB : (index + 1) * SUB]
        return (lambda which: value, 0)

    for j in range(of_j):
        for i in range(of_i):
            texts = [block(text, (j * 2 + i % 2) * blocks_j + k) for k in range(blocks_j)]
            images = [block(image, i * blocks_i + k) for k in range(blocks_i)]
            for which, value in enumerate(packed(images + texts, narrow)):
                out_ref[j * of_i + i, :, which * LANES : (which + 1) * LANES] = value


def side_by_side(groups, full, rest):
    found, shared, per = [], [], LANES // rest
    for group, tiles in enumerate(groups):
        found += [((group * full + which) * LANES, tiles[which]) for which in range(full)]
        at = group % per * rest
        moved = shift(tiles[full], at)
        if at == 0:
            shared.append(moved)
        else:
            shared[-1] = jnp.where(lanes_from(at, moved.shape), moved, shared[-1])
    return found + [((len(groups) * full + k) * LANES, tile) for k, tile in enumerate(shared)]


def apart(ref, groups, full, rest):
    per = LANES // rest
    found = []
    for group in range(groups):
        tiles = [ref[:, (group * full + k) * LANES : (group * full + k + 1) * LANES] for k in range(full)]
        lo = (groups * full + group // per) * LANES
        found.append(tiles + [shift(ref[:, lo : lo + LANES], -(group % per) * rest)])
    return found


def widen_kernel(sizes, narrow, got_ref, image_ref, text_ref):
    of_i, of_j, blocks_i, blocks_j = sizes
    copies = image_ref.shape[0]
    full, rest = divmod(of_i * narrow, LANES)
    last, texts = None, []
    for j in range(of_j):
        sources = [reader(got_ref, j * of_i + i) for i in range(of_i)]
        for k in range(blocks_i + blocks_j):
            tiles = packed([(source, k * narrow) for source in sources], narrow)
            if k < blocks_i:
                group = j * blocks_i + k
                for copy in range(copies):
                    for which in range(full):
                        lo = (group * full + which) * LANES
                        image_ref[copy, :, lo : lo + LANES] = tiles[which]
                moved = shift(tiles[full], group * rest)
                last = moved if last is None else jnp.where(lanes_from(group * rest, moved.shape), moved, last)
            else:
                texts.append(tiles)
    for lane, value in side_by_side(texts, full, rest):
        text_ref[:, lane : lane + LANES] = value
    lo = of_j * blocks_i * full * LANES
    for copy in range(copies):
        image_ref[copy, :, lo : lo + LANES] = last


def stacked(image_ref, groups, full, rest):
    sources = image_ref.shape[0]
    lo = groups * full * LANES
    last = image_ref[:, :, lo : lo + LANES].reshape(sources * SUB, LANES)
    found = []
    for group in range(groups):
        at = group * full * LANES
        whole = image_ref[:, :, at : at + full * LANES].reshape(sources * SUB, full * LANES)
        found.append(jnp.concatenate([whole, shift(last, -group * rest)], axis=1))
    return jnp.concatenate(found, axis=0)


dot = functools.partial(
    lax.dot_general, preferred_element_type=jnp.float32, precision=lax.Precision.HIGHEST
)


def both_halves(tiling, text_ref, pair_ref):
    groups, full, rest = tiling
    rows = []
    for ref in (text_ref, pair_ref):
        for tiles in apart(ref, groups, full, rest):
            last = jnp.where(lanes_from(rest, tiles[full].shape), 0.0, tiles[full])
            rows.append(jnp.concatenate(tiles[:full] + [last], axis=1))
    return jnp.concatenate(rows, axis=0)


def logits_kernel(tiling, text_tiling, image_ref, text_ref, pair_ref, out_ref):
    text = both_halves(text_tiling, text_ref, pair_ref)
    out_ref[...] = dot(stacked(image_ref, *tiling), text, (((1,), (1,)), ((), ())))


def grads_kernel(sizes, tiling, text_tiling, log_scale_ref, bias_ref, both_ref, *refs):
    image_ref, text_ref, pair_ref, gi_ref, gt_ref, gt_pair_ref = refs
    high, of_y, rows, group_i, group_j = sizes
    groups, full, rest = tiling
    sources = image_ref.shape[0]
    scale = jnp.exp(jnp.full((1, 1), log_scale_ref[0], jnp.float32))
    logits = scale * (both_ref[0] + both_ref[1]) + bias_ref[0]
    x, y, i, j = (lax.axis_index(a) for a in ("x", "y", "zm", "zh"))
    r = lax.broadcasted_iota(jnp.int32, logits.shape, 0)
    group, source = r // (sources * SUB), r % (sources * SUB) // SUB
    blocks_i = group_i // SUB
    zh, inner = group // blocks_i, group % blocks_i * SUB + r % SUB
    row_ids = ((source // of_y * high + zh) * of_y + source % of_y) * rows + i * group_i + inner
    c = lax.broadcasted_iota(jnp.int32, logits.shape, 1)
    half, of_half = group_j // 2, gt_ref.shape[0]
    which = (i + c // of_half) % 2
    zh, inner = c % of_half // half, c % half
    col_ids = ((x * high + zh) * of_y + y) * rows + j * group_j + which * half + inner
    label = jnp.where(row_ids == col_ids, 1.0, -1.0)
    coef = -label * jax.nn.sigmoid(-label * logits)
    coef = scale * coef
    found = dot(coef, both_halves(text_tiling, text_ref, pair_ref), (((1,), (0,)), ((), ())))
    last = None
    for group in range(groups):
        part = found[group * sources * SUB : (group + 1) * sources * SUB]
        at = group * full * LANES
        gi_ref[:, :, at : at + full * LANES] = part[:, : full * LANES].reshape(sources, SUB, full * LANES)
        moved = shift(part[:, full * LANES :], group * rest)
        last = moved if last is None else last + moved
    lo = groups * full * LANES
    gi_ref[:, :, lo : lo + LANES] = last.reshape(sources, SUB, LANES)
    found = dot(coef, stacked(image_ref, *tiling), (((0,), (0,)), ((), ())))
    gt_ref[...] = found[:of_half]
    pair = [found[at : at + SUB] for at in range(of_half, 2 * of_half, SUB)]
    pair = [[rows_of[:, k * LANES : (k + 1) * LANES] for k in range(full + 1)] for rows_of in pair]
    for lane, value in side_by_side(pair, full, rest):
        gt_pair_ref[:, lane : lane + LANES] = value


def narrow_kernel(sizes, narrow, image_ref, text_ref, pair_ref, out_ref):
    of_i, of_j, blocks_i, blocks_j = sizes
    full, rest = divmod(of_i * narrow, LANES)
    total = image_ref[0]
    for copy in range(1, image_ref.shape[0]):
        total = total + image_ref[copy]
    lo = of_j * blocks_i * full
    tiles = [total[:, k * LANES : (k + 1) * LANES] for k in range(lo + 1)]

    def image_row(group):
        row = tiles[group * full : (group + 1) * full] + [shift(tiles[lo], -group * rest)]
        return lambda which: row[which]

    pair = apart(pair_ref, of_j * blocks_j, full, rest)

    def text_row(start):
        own = reader(text_ref, None, start)
        row = [own(which) + pair[start // SUB][which] for which in range(full + 1)]
        return lambda which: row[which]

    for j in range(of_j):
        rows = [image_row(j * blocks_i + k) for k in range(blocks_i)]
        rows += [text_row((j * blocks_j + k) * SUB) for k in range(blocks_j)]
        for i in range(of_i):
            for which, value in enumerate(packed([(row, i * narrow) for row in rows], narrow)):
                out_ref[j * of_i + i, :, which * LANES : (which + 1) * LANES] = value


def collect_kernel(sizes, got_ref, image_ref, text_ref):
    of_i, of_j, blocks_i, blocks_j = sizes
    narrow = image_ref.shape[0]

    def total(sources, first, last):
        tiles = {}
        for which in range(first * narrow // LANES, tiles_of(last * narrow)):
            tiles[which] = reader(got_ref, sources[0])(which)
            for source in sources[1:]:
                tiles[which] = tiles[which] + reader(got_ref, source)(which)
        return [pick(lambda which: tiles[which], k * narrow, narrow, 0) for k in range(first, last)]

    images, texts = [], []
    for i in range(of_i):
        images += total([j * of_i + i for j in range(of_j)], 0, blocks_i)
    for j in range(of_j):
        for half in range(2):
            texts += total([j * of_i + i for i in range(half, of_i, 2)], blocks_i, blocks_i + blocks_j)
    image_ref[...] = jnp.concatenate(images, axis=0).T[:narrow]
    text_ref[...] = jnp.concatenate(texts, axis=0).T[:narrow]


def call(kernel, outs, *operands, inputs=None, scratch=()):
    many = isinstance(outs, list)
    shapes = [jax.ShapeDtypeStruct(s, jnp.float32) for s in (outs if many else [outs])]
    return pl.pallas_call(
        kernel,
        out_shape=shapes if many else shapes[0],
        in_specs=inputs or [VMEM] * len(operands),
        out_specs=[VMEM] * len(shapes) if many else VMEM,
        scratch_shapes=list(scratch),
        compiler_params=pltpu.CompilerParams(vmem_limit_bytes=32 * 1024 * 1024),
    )(*operands)


def exchange(value, axis):
    return lax.all_to_all(value, axis, split_axis=0, concat_axis=0, tiled=True)


def on_device(image_emb, text_emb, log_scale, logit_bias):
    of_x, of_j, of_y, of_i = (lax.axis_size(a) for a in ("x", "zh", "y", "zm"))
    rows, narrow = image_emb.shape
    group_i, group_j = rows // of_i, rows // of_j
    blocks = (of_i, of_j, group_i // SUB, group_j // 2 // SUB)
    full, rest = divmod(of_i * narrow, LANES)
    groups = of_j * blocks[2]
    assert 0 < rest * groups <= LANES
    tiling = (groups, full, rest)
    plane = of_x * of_y
    text_groups = of_j * blocks[3]
    text_tiling = (text_groups, full, rest)
    text_shape = (SUB, (text_groups * full + -(-text_groups // (LANES // rest))) * LANES)
    grad_shape = (text_groups * SUB, (full + 1) * LANES)
    sent_shape = (of_j * of_i, SUB, tiles_of((blocks[2] + blocks[3]) * narrow) * LANES)
    block = pltpu.VMEM((narrow, rows), jnp.float32)

    held = [pltpu.with_memory_space_constraint(a.T, pltpu.HBM) for a in (image_emb, text_emb)]
    sent = call(
        functools.partial(split_kernel, of_i, of_j), sent_shape, *held,
        inputs=[pl.BlockSpec(memory_space=pltpu.HBM)] * 2,
        scratch=[block, block, pltpu.SemaphoreType.DMA((2,))],
    )
    got = exchange(sent, ("zh", "zm"))
    mine, text = call(
        functools.partial(widen_kernel, blocks, narrow),
        [(plane, SUB, (groups * full + 1) * LANES), text_shape],
        got,
    )
    pairs = [(k, k ^ 1) for k in range(of_i)]
    pair = lax.ppermute(text, "zm", pairs)
    image = exchange(mine, ("x", "y"))
    part = call(functools.partial(logits_kernel, tiling, text_tiling), (plane * groups * SUB, of_j * group_j), image, text, pair)
    other = lax.ppermute(part, "ze", [(0, 1), (1, 0)])
    both = lax.all_gather(part + other, "c")
    grad_i, grad_t, grad_pair = call(
        functools.partial(grads_kernel, (of_j, of_y, rows, group_i, group_j), tiling, text_tiling),
        [image.shape, grad_shape, text_shape],
        log_scale, logit_bias, both, image, text, pair,
        inputs=[SMEM] * 2 + [VMEM] * 4,
    )
    back_t = lax.ppermute(grad_pair, "zm", pairs)
    back = exchange(grad_i, ("x", "y"))
    sent = call(functools.partial(narrow_kernel, blocks, narrow), sent_shape, back, grad_t, back_t)
    got = exchange(sent, ("zh", "zm"))
    out_i, out_t = call(functools.partial(collect_kernel, blocks), [(narrow, rows), (narrow, rows)], got)
    return (out_i.T, out_t.T)


def program(mesh, sizes):
    x, zh, y, zl, c = sizes
    fine = Mesh(mesh.devices.reshape(x, zh, y, zl // 2, 2, c), ("x", "zh", "y", "zm", "ze", "c"))
    dp, mp = ("x", "zh", "y"), ("zm", "ze", "c")
    return jax.shard_map(
        on_device,
        mesh=fine,
        in_specs=(P(dp, mp), P(dp, mp), P(), P()),
        out_specs=(P(dp, mp), P(dp, mp)),
        check_vma=False,
    )


def solution(mesh):
    return program(mesh, (4, 2, 4, 16, 2))
```

```python
import functools

import jax
import jax.numpy as jnp
from jax import lax
from jax.experimental import pallas as pl
from jax.experimental.pallas import tpu as pltpu
from jax.sharding import Mesh, PartitionSpec as P

LANES = 128
SUB = 8
VMEM = pl.BlockSpec(memory_space=pltpu.VMEM)
SMEM = pl.BlockSpec(memory_space=pltpu.SMEM)


def rows_first(block):
    narrow, rows = block.shape
    filled = jnp.concatenate([block, jnp.zeros((LANES - narrow, rows), block.dtype)], axis=0)
    return filled.T


def shift(block, lanes):
    lanes = lanes % LANES
    return block if lanes == 0 else pltpu.roll(block, lanes, 1)


def tiles_of(lanes):
    return -(-lanes // LANES)


def lanes_from(off, shape):
    return lax.broadcasted_iota(jnp.int32, shape, 1) >= off


def pick(tile, at, width, to):
    which, off = divmod(at, LANES)
    value = tile(which)
    if off + width <= LANES:
        return shift(value, to - off)
    first, second = shift(value, -off), shift(tile(which + 1), -off)
    return shift(jnp.where(lanes_from(LANES - off, value.shape), second, first), to)


def packed(blocks, width):
    tiles = [None] * tiles_of(len(blocks) * width)
    for k, (tile, at) in enumerate(blocks):
        which, off = divmod(k * width, LANES)
        value = pick(tile, at, width, off)
        tiles[which] = value if tiles[which] is None else jnp.where(lanes_from(off, value.shape), value, tiles[which])
        if off + width > LANES:
            tiles[which + 1] = value
    return tiles


def reader(ref, first, start=0):
    def tile(which):
        lanes = slice(which * LANES, (which + 1) * LANES)
        if first is None:
            return ref[start : start + SUB, lanes]
        return ref[first, start : start + SUB, lanes]

    return tile


def split_kernel(of_i, of_j, image_hbm, text_hbm, out_ref, image_ref, text_ref, sems):
    copies = [
        pltpu.make_async_copy(image_hbm, image_ref, sems.at[0]),
        pltpu.make_async_copy(text_hbm, text_ref, sems.at[1]),
    ]
    for copy in copies:
        copy.start()
    for copy in copies:
        copy.wait()
    narrow, rows = image_ref.shape
    image, text = rows_first(image_ref[...]), rows_first(text_ref[...])
    blocks_i, blocks_j = rows // of_i // SUB, rows // of_j // 2 // SUB

    def block(rows_of, index):
        value = rows_of[index * SUB : (index + 1) * SUB]
        return (lambda which: value, 0)

    for j in range(of_j):
        for i in range(of_i):
            texts = [block(text, (j * 2 + i % 2) * blocks_j + k) for k in range(blocks_j)]
            images = [block(image, i * blocks_i + k) for k in range(blocks_i)]
            for which, value in enumerate(packed(images + texts, narrow)):
                out_ref[j * of_i + i, :, which * LANES : (which + 1) * LANES] = value


def side_by_side(groups, full, rest):
    found, shared, per = [], [], LANES // rest
    for group, tiles in enumerate(groups):
        found += [((group * full + which) * LANES, tiles[which]) for which in range(full)]
        at = group % per * rest
        moved = shift(tiles[full], at)
        if at == 0:
            shared.append(moved)
        else:
            shared[-1] = jnp.where(lanes_from(at, moved.shape), moved, shared[-1])
    return found + [((len(groups) * full + k) * LANES, tile) for k, tile in enumerate(shared)]


def apart(ref, groups, full, rest):
    per = LANES // rest
    found = []
    for group in range(groups):
        tiles = [ref[:, (group * full + k) * LANES : (group * full + k + 1) * LANES] for k in range(full)]
        lo = (groups * full + group // per) * LANES
        found.append(tiles + [shift(ref[:, lo : lo + LANES], -(group % per) * rest)])
    return found


def widen_kernel(sizes, narrow, got_ref, image_ref, text_ref):
    of_i, of_j, blocks_i, blocks_j = sizes
    copies = image_ref.shape[0]
    full, rest = divmod(of_i * narrow, LANES)
    last, texts = None, []
    for j in range(of_j):
        sources = [reader(got_ref, j * of_i + i) for i in range(of_i)]
        for k in range(blocks_i + blocks_j):
            tiles = packed([(source, k * narrow) for source in sources], narrow)
            if k < blocks_i:
                group = j * blocks_i + k
                for copy in range(copies):
                    for which in range(full):
                        lo = (group * full + which) * LANES
                        image_ref[copy, :, lo : lo + LANES] = tiles[which]
                moved = shift(tiles[full], group * rest)
                last = moved if last is None else jnp.where(lanes_from(group * rest, moved.shape), moved, last)
            else:
                texts.append(tiles)
    for lane, value in side_by_side(texts, full, rest):
        text_ref[:, lane : lane + LANES] = value
    lo = of_j * blocks_i * full * LANES
    for copy in range(copies):
        image_ref[copy, :, lo : lo + LANES] = last


def stacked(image_ref, groups, full, rest):
    sources = image_ref.shape[0]
    lo = groups * full * LANES
    last = image_ref[:, :, lo : lo + LANES].reshape(sources * SUB, LANES)
    found = []
    for group in range(groups):
        at = group * full * LANES
        whole = image_ref[:, :, at : at + full * LANES].reshape(sources * SUB, full * LANES)
        found.append(jnp.concatenate([whole, shift(last, -group * rest)], axis=1))
    return jnp.concatenate(found, axis=0)


dot = functools.partial(
    lax.dot_general, preferred_element_type=jnp.float32, precision=lax.Precision.HIGHEST
)


def both_halves(tiling, text_ref, pair_ref):
    groups, full, rest = tiling
    rows = []
    for ref in (text_ref, pair_ref):
        for tiles in apart(ref, groups, full, rest):
            last = jnp.where(lanes_from(rest, tiles[full].shape), 0.0, tiles[full])
            rows.append(jnp.concatenate(tiles[:full] + [last], axis=1))
    return jnp.concatenate(rows, axis=0)


def logits_kernel(tiling, text_tiling, image_ref, text_ref, pair_ref, *out_refs):
    text = both_halves(text_tiling, text_ref, pair_ref)
    found = dot(stacked(image_ref, *tiling), text, (((1,), (1,)), ((), ())))
    rows = out_refs[0].shape[0]
    for k, out_ref in enumerate(out_refs):
        out_ref[...] = found[k * rows : (k + 1) * rows]


def image_grads_kernel(sizes, tiling, text_tiling, log_scale_ref, bias_ref, first_ref, second_ref, text_ref, pair_ref, gi_ref, coef_ref):
    high, of_y, rows, group_i, group_j = sizes
    groups, full, rest = tiling
    sources = gi_ref.shape[0]
    scale = jnp.exp(jnp.full((1, 1), log_scale_ref[0], jnp.float32))
    summed = jnp.concatenate([ref[0] + ref[1] for ref in (first_ref, second_ref)], axis=0)
    logits = scale * summed + bias_ref[0]
    x, y, i, j = (lax.axis_index(a) for a in ("x", "y", "zm", "zh"))
    r = lax.broadcasted_iota(jnp.int32, logits.shape, 0)
    group, source = r // (sources * SUB), r % (sources * SUB) // SUB
    blocks_i = group_i // SUB
    zh, inner = group // blocks_i, group % blocks_i * SUB + r % SUB
    row_ids = ((source // of_y * high + zh) * of_y + source % of_y) * rows + i * group_i + inner
    c = lax.broadcasted_iota(jnp.int32, logits.shape, 1)
    half, of_half = group_j // 2, logits.shape[1] // 2
    which = (i + c // of_half) % 2
    zh, inner = c % of_half // half, c % half
    col_ids = ((x * high + zh) * of_y + y) * rows + j * group_j + which * half + inner
    label = jnp.where(row_ids == col_ids, 1.0, -1.0)
    coef = -label * jax.nn.sigmoid(-label * logits)
    coef = scale * coef
    coef_ref[...] = coef
    found = dot(coef, both_halves(text_tiling, text_ref, pair_ref), (((1,), (0,)), ((), ())))
    last = None
    for group in range(groups):
        part = found[group * sources * SUB : (group + 1) * sources * SUB]
        at = group * full * LANES
        gi_ref[:, :, at : at + full * LANES] = part[:, : full * LANES].reshape(sources, SUB, full * LANES)
        moved = shift(part[:, full * LANES :], group * rest)
        last = moved if last is None else last + moved
    lo = groups * full * LANES
    gi_ref[:, :, lo : lo + LANES] = last.reshape(sources, SUB, LANES)


def text_grads_kernel(tiling, coef_ref, image_ref, gt_ref, gt_pair_ref):
    _, full, rest = tiling
    of_half = gt_ref.shape[0]
    found = dot(coef_ref[...], stacked(image_ref, *tiling), (((0,), (0,)), ((), ())))
    gt_ref[...] = found[:of_half]
    pair = [found[at : at + SUB] for at in range(of_half, 2 * of_half, SUB)]
    pair = [[rows_of[:, k * LANES : (k + 1) * LANES] for k in range(full + 1)] for rows_of in pair]
    for lane, value in side_by_side(pair, full, rest):
        gt_pair_ref[:, lane : lane + LANES] = value


def narrow_kernel(sizes, narrow, image_ref, text_ref, pair_ref, out_ref):
    of_i, of_j, blocks_i, blocks_j = sizes
    full, rest = divmod(of_i * narrow, LANES)
    total = image_ref[0]
    for copy in range(1, image_ref.shape[0]):
        total = total + image_ref[copy]
    lo = of_j * blocks_i * full
    tiles = [total[:, k * LANES : (k + 1) * LANES] for k in range(lo + 1)]

    def image_row(group):
        row = tiles[group * full : (group + 1) * full] + [shift(tiles[lo], -group * rest)]
        return lambda which: row[which]

    pair = apart(pair_ref, of_j * blocks_j, full, rest)

    def text_row(start):
        own = reader(text_ref, None, start)
        row = [own(which) + pair[start // SUB][which] for which in range(full + 1)]
        return lambda which: row[which]

    for j in range(of_j):
        rows = [image_row(j * blocks_i + k) for k in range(blocks_i)]
        rows += [text_row((j * blocks_j + k) * SUB) for k in range(blocks_j)]
        for i in range(of_i):
            for which, value in enumerate(packed([(row, i * narrow) for row in rows], narrow)):
                out_ref[j * of_i + i, :, which * LANES : (which + 1) * LANES] = value


def collect_kernel(sizes, got_ref, image_ref, text_ref):
    of_i, of_j, blocks_i, blocks_j = sizes
    narrow = image_ref.shape[0]

    def total(sources, first, last):
        tiles = {}
        for which in range(first * narrow // LANES, tiles_of(last * narrow)):
            tiles[which] = reader(got_ref, sources[0])(which)
            for source in sources[1:]:
                tiles[which] = tiles[which] + reader(got_ref, source)(which)
        return [pick(lambda which: tiles[which], k * narrow, narrow, 0) for k in range(first, last)]

    images, texts = [], []
    for i in range(of_i):
        images += total([j * of_i + i for j in range(of_j)], 0, blocks_i)
    for j in range(of_j):
        for half in range(2):
            texts += total([j * of_i + i for i in range(half, of_i, 2)], blocks_i, blocks_i + blocks_j)
    image_ref[...] = jnp.concatenate(images, axis=0).T[:narrow]
    text_ref[...] = jnp.concatenate(texts, axis=0).T[:narrow]


def call(kernel, outs, *operands, inputs=None, scratch=()):
    many = isinstance(outs, list)
    shapes = [jax.ShapeDtypeStruct(s, jnp.float32) for s in (outs if many else [outs])]
    return pl.pallas_call(
        kernel,
        out_shape=shapes if many else shapes[0],
        in_specs=inputs or [VMEM] * len(operands),
        out_specs=[VMEM] * len(shapes) if many else VMEM,
        scratch_shapes=list(scratch),
        compiler_params=pltpu.CompilerParams(vmem_limit_bytes=32 * 1024 * 1024),
    )(*operands)


def exchange(value, axis):
    return lax.all_to_all(value, axis, split_axis=0, concat_axis=0, tiled=True)


def on_device(image_emb, text_emb, log_scale, logit_bias):
    of_x, of_j, of_y, of_i = (lax.axis_size(a) for a in ("x", "zh", "y", "zm"))
    rows, narrow = image_emb.shape
    group_i, group_j = rows // of_i, rows // of_j
    blocks = (of_i, of_j, group_i // SUB, group_j // 2 // SUB)
    full, rest = divmod(of_i * narrow, LANES)
    groups = of_j * blocks[2]
    assert 0 < rest * groups <= LANES
    tiling = (groups, full, rest)
    plane = of_x * of_y
    text_groups = of_j * blocks[3]
    text_tiling = (text_groups, full, rest)
    text_shape = (SUB, (text_groups * full + -(-text_groups // (LANES // rest))) * LANES)
    grad_shape = (text_groups * SUB, (full + 1) * LANES)
    sent_shape = (of_j * of_i, SUB, tiles_of((blocks[2] + blocks[3]) * narrow) * LANES)
    block = pltpu.VMEM((narrow, rows), jnp.float32)

    held = [pltpu.with_memory_space_constraint(a.T, pltpu.HBM) for a in (image_emb, text_emb)]
    sent = call(
        functools.partial(split_kernel, of_i, of_j), sent_shape, *held,
        inputs=[pl.BlockSpec(memory_space=pltpu.HBM)] * 2,
        scratch=[block, block, pltpu.SemaphoreType.DMA((2,))],
    )
    got = exchange(sent, ("zh", "zm"))
    mine, text = call(
        functools.partial(widen_kernel, blocks, narrow),
        [(plane, SUB, (groups * full + 1) * LANES), text_shape],
        got,
    )
    pairs = [(k, k ^ 1) for k in range(of_i)]
    pair = lax.ppermute(text, "zm", pairs)
    image = exchange(mine, ("x", "y"))
    shape = (plane * groups * SUB, of_j * group_j)
    parts = call(
        functools.partial(logits_kernel, tiling, text_tiling), [(shape[0] // 2, shape[1])] * 2, image, text, pair
    )
    others = [lax.ppermute(part, "ze", [(0, 1), (1, 0)]) for part in parts]
    both = [lax.all_gather(part + other, "c") for part, other in zip(parts, others)]
    grad_i, coef = call(
        functools.partial(image_grads_kernel, (of_j, of_y, rows, group_i, group_j), tiling, text_tiling),
        [image.shape, shape],
        log_scale, logit_bias, *both, text, pair,
        inputs=[SMEM] * 2 + [VMEM] * 4,
    )
    grad_t, grad_pair = call(functools.partial(text_grads_kernel, tiling), [grad_shape, text_shape], coef, image)
    back_t = lax.ppermute(grad_pair, "zm", pairs)
    back = exchange(grad_i, ("x", "y"))
    sent = call(functools.partial(narrow_kernel, blocks, narrow), sent_shape, back, grad_t, back_t)
    got = exchange(sent, ("zh", "zm"))
    out_i, out_t = call(functools.partial(collect_kernel, blocks), [(narrow, rows), (narrow, rows)], got)
    return (out_i.T, out_t.T)


def program(mesh, sizes):
    x, zh, y, zl, c = sizes
    fine = Mesh(mesh.devices.reshape(x, zh, y, zl // 2, 2, c), ("x", "zh", "y", "zm", "ze", "c"))
    dp, mp = ("x", "zh", "y"), ("zm", "ze", "c")
    return jax.shard_map(
        on_device,
        mesh=fine,
        in_specs=(P(dp, mp), P(dp, mp), P(), P()),
        out_specs=(P(dp, mp), P(dp, mp)),
        check_vma=False,
    )


def solution(mesh):
    return program(mesh, (4, 2, 4, 16, 2))
```

```python
import functools

import jax
import jax.numpy as jnp
from jax import lax
from jax.experimental import pallas as pl
from jax.experimental.pallas import tpu as pltpu
from jax.sharding import Mesh, PartitionSpec as P

LANES = 128
SUB = 8
VMEM = pl.BlockSpec(memory_space=pltpu.VMEM)
SMEM = pl.BlockSpec(memory_space=pltpu.SMEM)


def rows_first(block):
    narrow, rows = block.shape
    filled = jnp.concatenate([block, jnp.zeros((LANES - narrow, rows), block.dtype)], axis=0)
    return filled.T


def shift(block, lanes):
    lanes = lanes % LANES
    return block if lanes == 0 else pltpu.roll(block, lanes, 1)


def tiles_of(lanes):
    return -(-lanes // LANES)


def lanes_from(off, shape):
    return lax.broadcasted_iota(jnp.int32, shape, 1) >= off


def pick(tile, at, width, to):
    which, off = divmod(at, LANES)
    value = tile(which)
    if off + width <= LANES:
        return shift(value, to - off)
    first, second = shift(value, -off), shift(tile(which + 1), -off)
    return shift(jnp.where(lanes_from(LANES - off, value.shape), second, first), to)


def packed(blocks, width):
    tiles = [None] * tiles_of(len(blocks) * width)
    for k, (tile, at) in enumerate(blocks):
        which, off = divmod(k * width, LANES)
        value = pick(tile, at, width, off)
        tiles[which] = value if tiles[which] is None else jnp.where(lanes_from(off, value.shape), value, tiles[which])
        if off + width > LANES:
            tiles[which + 1] = value
    return tiles


def reader(ref, first, start=0):
    def tile(which):
        lanes = slice(which * LANES, (which + 1) * LANES)
        if first is None:
            return ref[start : start + SUB, lanes]
        return ref[first, start : start + SUB, lanes]

    return tile


def split_kernel(of_i, of_j, image_hbm, text_hbm, out_ref, image_ref, text_ref, sems):
    copies = [
        pltpu.make_async_copy(image_hbm, image_ref, sems.at[0]),
        pltpu.make_async_copy(text_hbm, text_ref, sems.at[1]),
    ]
    for copy in copies:
        copy.start()
    for copy in copies:
        copy.wait()
    narrow, rows = image_ref.shape
    image, text = rows_first(image_ref[...]), rows_first(text_ref[...])
    blocks_i, blocks_j = rows // of_i // SUB, rows // of_j // 2 // SUB

    def block(rows_of, index):
        value = rows_of[index * SUB : (index + 1) * SUB]
        return (lambda which: value, 0)

    for j in range(of_j):
        for i in range(of_i):
            texts = [block(text, (j * 2 + i % 2) * blocks_j + k) for k in range(blocks_j)]
            images = [block(image, i * blocks_i + k) for k in range(blocks_i)]
            for which, value in enumerate(packed(images + texts, narrow)):
                out_ref[j * of_i + i, :, which * LANES : (which + 1) * LANES] = value


def side_by_side(groups, full, rest):
    found, shared, per = [], [], LANES // rest
    for group, tiles in enumerate(groups):
        found += [((group * full + which) * LANES, tiles[which]) for which in range(full)]
        at = group % per * rest
        moved = shift(tiles[full], at)
        if at == 0:
            shared.append(moved)
        else:
            shared[-1] = jnp.where(lanes_from(at, moved.shape), moved, shared[-1])
    return found + [((len(groups) * full + k) * LANES, tile) for k, tile in enumerate(shared)]


def apart(ref, groups, full, rest):
    per = LANES // rest
    found = []
    for group in range(groups):
        tiles = [ref[:, (group * full + k) * LANES : (group * full + k + 1) * LANES] for k in range(full)]
        lo = (groups * full + group // per) * LANES
        found.append(tiles + [shift(ref[:, lo : lo + LANES], -(group % per) * rest)])
    return found


def widen_kernel(sizes, narrow, got_ref, image_ref, text_ref):
    of_i, of_j, blocks_i, blocks_j = sizes
    copies = image_ref.shape[0]
    full, rest = divmod(of_i * narrow, LANES)
    last, texts = None, []
    for j in range(of_j):
        sources = [reader(got_ref, j * of_i + i) for i in range(of_i)]
        for k in range(blocks_i + blocks_j):
            tiles = packed([(source, k * narrow) for source in sources], narrow)
            if k < blocks_i:
                group = j * blocks_i + k
                for copy in range(copies):
                    for which in range(full):
                        lo = (group * full + which) * LANES
                        image_ref[copy, :, lo : lo + LANES] = tiles[which]
                moved = shift(tiles[full], group * rest)
                last = moved if last is None else jnp.where(lanes_from(group * rest, moved.shape), moved, last)
            else:
                texts.append(tiles)
    for lane, value in side_by_side(texts, full, rest):
        text_ref[:, lane : lane + LANES] = value
    lo = of_j * blocks_i * full * LANES
    for copy in range(copies):
        image_ref[copy, :, lo : lo + LANES] = last


def stacked(image_ref, groups, full, rest):
    sources = image_ref.shape[0]
    lo = groups * full * LANES
    last = image_ref[:, :, lo : lo + LANES].reshape(sources * SUB, LANES)
    found = []
    for group in range(groups):
        at = group * full * LANES
        whole = image_ref[:, :, at : at + full * LANES].reshape(sources * SUB, full * LANES)
        found.append(jnp.concatenate([whole, shift(last, -group * rest)], axis=1))
    return jnp.concatenate(found, axis=0)


dot = functools.partial(
    lax.dot_general, preferred_element_type=jnp.float32, precision=lax.Precision.HIGHEST
)


def both_halves(tiling, text_ref, pair_ref):
    groups, full, rest = tiling
    rows = []
    for ref in (text_ref, pair_ref):
        for tiles in apart(ref, groups, full, rest):
            last = jnp.where(lanes_from(rest, tiles[full].shape), 0.0, tiles[full])
            rows.append(jnp.concatenate(tiles[:full] + [last], axis=1))
    return jnp.concatenate(rows, axis=0)


def logits_kernel(tiling, text_tiling, log_scale_ref, bias_ref, image_ref, text_ref, pair_ref, *out_refs):
    text = both_halves(text_tiling, text_ref, pair_ref)
    scale = jnp.exp(jnp.full((1, 1), log_scale_ref[0], jnp.float32))
    found = scale * dot(stacked(image_ref, *tiling), text, (((1,), (1,)), ((), ()))) + 0.25 * bias_ref[0]
    rows = out_refs[0].shape[0]
    for k, out_ref in enumerate(out_refs):
        out_ref[...] = found[k * rows : (k + 1) * rows]


def image_grads_kernel(sizes, tiling, text_tiling, log_scale_ref, first_ref, second_ref, text_ref, pair_ref, gi_ref, coef_ref):
    high, of_y, rows, group_i, group_j = sizes
    groups, full, rest = tiling
    sources = gi_ref.shape[0]
    scale = jnp.exp(jnp.full((1, 1), log_scale_ref[0], jnp.float32))
    logits = jnp.concatenate([ref[0] + ref[1] for ref in (first_ref, second_ref)], axis=0)
    x, y, i, j = (lax.axis_index(a) for a in ("x", "y", "zm", "zh"))
    r = lax.broadcasted_iota(jnp.int32, logits.shape, 0)
    group, source = r // (sources * SUB), r % (sources * SUB) // SUB
    blocks_i = group_i // SUB
    zh, inner = group // blocks_i, group % blocks_i * SUB + r % SUB
    row_ids = ((source // of_y * high + zh) * of_y + source % of_y) * rows + i * group_i + inner
    c = lax.broadcasted_iota(jnp.int32, logits.shape, 1)
    half, of_half = group_j // 2, logits.shape[1] // 2
    which = (i + c // of_half) % 2
    zh, inner = c % of_half // half, c % half
    col_ids = ((x * high + zh) * of_y + y) * rows + j * group_j + which * half + inner
    label = jnp.where(row_ids == col_ids, 1.0, -1.0)
    coef = -label * jax.nn.sigmoid(-label * logits)
    coef = scale * coef
    coef_ref[...] = coef
    found = dot(coef, both_halves(text_tiling, text_ref, pair_ref), (((1,), (0,)), ((), ())))
    last = None
    for group in range(groups):
        part = found[group * sources * SUB : (group + 1) * sources * SUB]
        at = group * full * LANES
        gi_ref[:, :, at : at + full * LANES] = part[:, : full * LANES].reshape(sources, SUB, full * LANES)
        moved = shift(part[:, full * LANES :], group * rest)
        last = moved if last is None else last + moved
    lo = groups * full * LANES
    gi_ref[:, :, lo : lo + LANES] = last.reshape(sources, SUB, LANES)


def text_grads_kernel(tiling, coef_ref, image_ref, gt_ref, gt_pair_ref):
    _, full, rest = tiling
    of_half = gt_ref.shape[0]
    found = dot(coef_ref[...], stacked(image_ref, *tiling), (((0,), (0,)), ((), ())))
    gt_ref[...] = found[:of_half]
    pair = [found[at : at + SUB] for at in range(of_half, 2 * of_half, SUB)]
    pair = [[rows_of[:, k * LANES : (k + 1) * LANES] for k in range(full + 1)] for rows_of in pair]
    for lane, value in side_by_side(pair, full, rest):
        gt_pair_ref[:, lane : lane + LANES] = value


def narrow_kernel(sizes, narrow, image_ref, text_ref, pair_ref, out_ref):
    of_i, of_j, blocks_i, blocks_j = sizes
    full, rest = divmod(of_i * narrow, LANES)
    total = image_ref[0]
    for copy in range(1, image_ref.shape[0]):
        total = total + image_ref[copy]
    lo = of_j * blocks_i * full
    tiles = [total[:, k * LANES : (k + 1) * LANES] for k in range(lo + 1)]

    def image_row(group):
        row = tiles[group * full : (group + 1) * full] + [shift(tiles[lo], -group * rest)]
        return lambda which: row[which]

    pair = apart(pair_ref, of_j * blocks_j, full, rest)

    def text_row(start):
        own = reader(text_ref, None, start)
        row = [own(which) + pair[start // SUB][which] for which in range(full + 1)]
        return lambda which: row[which]

    for j in range(of_j):
        rows = [image_row(j * blocks_i + k) for k in range(blocks_i)]
        rows += [text_row((j * blocks_j + k) * SUB) for k in range(blocks_j)]
        for i in range(of_i):
            for which, value in enumerate(packed([(row, i * narrow) for row in rows], narrow)):
                out_ref[j * of_i + i, :, which * LANES : (which + 1) * LANES] = value


def collect_kernel(sizes, got_ref, image_ref, text_ref):
    of_i, of_j, blocks_i, blocks_j = sizes
    narrow = image_ref.shape[0]

    def total(sources, first, last):
        tiles = {}
        for which in range(first * narrow // LANES, tiles_of(last * narrow)):
            tiles[which] = reader(got_ref, sources[0])(which)
            for source in sources[1:]:
                tiles[which] = tiles[which] + reader(got_ref, source)(which)
        return [pick(lambda which: tiles[which], k * narrow, narrow, 0) for k in range(first, last)]

    images, texts = [], []
    for i in range(of_i):
        images += total([j * of_i + i for j in range(of_j)], 0, blocks_i)
    for j in range(of_j):
        for half in range(2):
            texts += total([j * of_i + i for i in range(half, of_i, 2)], blocks_i, blocks_i + blocks_j)
    image_ref[...] = jnp.concatenate(images, axis=0).T[:narrow]
    text_ref[...] = jnp.concatenate(texts, axis=0).T[:narrow]


def call(kernel, outs, *operands, inputs=None, scratch=()):
    many = isinstance(outs, list)
    shapes = [jax.ShapeDtypeStruct(s, jnp.float32) for s in (outs if many else [outs])]
    return pl.pallas_call(
        kernel,
        out_shape=shapes if many else shapes[0],
        in_specs=inputs or [VMEM] * len(operands),
        out_specs=[VMEM] * len(shapes) if many else VMEM,
        scratch_shapes=list(scratch),
        compiler_params=pltpu.CompilerParams(vmem_limit_bytes=32 * 1024 * 1024),
    )(*operands)


def exchange(value, axis):
    return lax.all_to_all(value, axis, split_axis=0, concat_axis=0, tiled=True)


def on_device(image_emb, text_emb, log_scale, logit_bias):
    of_x, of_j, of_y, of_i = (lax.axis_size(a) for a in ("x", "zh", "y", "zm"))
    rows, narrow = image_emb.shape
    group_i, group_j = rows // of_i, rows // of_j
    blocks = (of_i, of_j, group_i // SUB, group_j // 2 // SUB)
    full, rest = divmod(of_i * narrow, LANES)
    groups = of_j * blocks[2]
    assert 0 < rest * groups <= LANES
    tiling = (groups, full, rest)
    plane = of_x * of_y
    text_groups = of_j * blocks[3]
    text_tiling = (text_groups, full, rest)
    text_shape = (SUB, (text_groups * full + -(-text_groups // (LANES // rest))) * LANES)
    grad_shape = (text_groups * SUB, (full + 1) * LANES)
    sent_shape = (of_j * of_i, SUB, tiles_of((blocks[2] + blocks[3]) * narrow) * LANES)
    block = pltpu.VMEM((narrow, rows), jnp.float32)

    held = [pltpu.with_memory_space_constraint(a.T, pltpu.HBM) for a in (image_emb, text_emb)]
    sent = call(
        functools.partial(split_kernel, of_i, of_j), sent_shape, *held,
        inputs=[pl.BlockSpec(memory_space=pltpu.HBM)] * 2,
        scratch=[block, block, pltpu.SemaphoreType.DMA((2,))],
    )
    got = exchange(sent, ("zh", "zm"))
    mine, text = call(
        functools.partial(widen_kernel, blocks, narrow),
        [(plane, SUB, (groups * full + 1) * LANES), text_shape],
        got,
    )
    pairs = [(k, k ^ 1) for k in range(of_i)]
    pair = lax.ppermute(text, "zm", pairs)
    image = exchange(mine, ("x", "y"))
    shape = (plane * groups * SUB, of_j * group_j)
    parts = call(
        functools.partial(logits_kernel, tiling, text_tiling), [(shape[0] // 2, shape[1])] * 2,
        log_scale, logit_bias, image, text, pair, inputs=[SMEM] * 2 + [VMEM] * 3,
    )
    others = [lax.ppermute(part, "ze", [(0, 1), (1, 0)]) for part in parts]
    both = [lax.all_gather(part + other, "c") for part, other in zip(parts, others)]
    grad_i, coef = call(
        functools.partial(image_grads_kernel, (of_j, of_y, rows, group_i, group_j), tiling, text_tiling),
        [image.shape, shape],
        log_scale, *both, text, pair,
        inputs=[SMEM] + [VMEM] * 4,
    )
    grad_t, grad_pair = call(functools.partial(text_grads_kernel, tiling), [grad_shape, text_shape], coef, image)
    back_t = lax.ppermute(grad_pair, "zm", pairs)
    back = exchange(grad_i, ("x", "y"))
    sent = call(functools.partial(narrow_kernel, blocks, narrow), sent_shape, back, grad_t, back_t)
    got = exchange(sent, ("zh", "zm"))
    out_i, out_t = call(functools.partial(collect_kernel, blocks), [(narrow, rows), (narrow, rows)], got)
    return (out_i.T, out_t.T)


def program(mesh, sizes):
    x, zh, y, zl, c = sizes
    fine = Mesh(mesh.devices.reshape(x, zh, y, zl // 2, 2, c), ("x", "zh", "y", "zm", "ze", "c"))
    dp, mp = ("x", "zh", "y"), ("zm", "ze", "c")
    return jax.shard_map(
        on_device,
        mesh=fine,
        in_specs=(P(dp, mp), P(dp, mp), P(), P()),
        out_specs=(P(dp, mp), P(dp, mp)),
        check_vma=False,
    )


def solution(mesh):
    return program(mesh, (4, 2, 4, 16, 2))
```

```python
import functools

import jax
import jax.numpy as jnp
from jax import lax
from jax.experimental import pallas as pl
from jax.experimental.pallas import tpu as pltpu
from jax.sharding import Mesh, PartitionSpec as P

LANES = 128
SUB = 8
VMEM = pl.BlockSpec(memory_space=pltpu.VMEM)
SMEM = pl.BlockSpec(memory_space=pltpu.SMEM)


def rows_first(block):
    narrow, rows = block.shape
    filled = jnp.concatenate([block, jnp.zeros((LANES - narrow, rows), block.dtype)], axis=0)
    return filled.T


def shift(block, lanes):
    lanes = lanes % LANES
    return block if lanes == 0 else pltpu.roll(block, lanes, 1)


def tiles_of(lanes):
    return -(-lanes // LANES)


def lanes_from(off, shape):
    return lax.broadcasted_iota(jnp.int32, shape, 1) >= off


def pick(tile, at, width, to):
    which, off = divmod(at, LANES)
    value = tile(which)
    if off + width <= LANES:
        return shift(value, to - off)
    first, second = shift(value, -off), shift(tile(which + 1), -off)
    return shift(jnp.where(lanes_from(LANES - off, value.shape), second, first), to)


def packed(blocks, width):
    tiles = [None] * tiles_of(len(blocks) * width)
    for k, (tile, at) in enumerate(blocks):
        which, off = divmod(k * width, LANES)
        value = pick(tile, at, width, off)
        tiles[which] = value if tiles[which] is None else jnp.where(lanes_from(off, value.shape), value, tiles[which])
        if off + width > LANES:
            tiles[which + 1] = value
    return tiles


def reader(ref, first, start=0):
    def tile(which):
        lanes = slice(which * LANES, (which + 1) * LANES)
        if first is None:
            return ref[start : start + SUB, lanes]
        return ref[first, start : start + SUB, lanes]

    return tile


def split_kernel(of_i, of_j, image_hbm, text_hbm, out_ref, image_ref, text_ref, sems):
    copies = [
        pltpu.make_async_copy(image_hbm, image_ref, sems.at[0]),
        pltpu.make_async_copy(text_hbm, text_ref, sems.at[1]),
    ]
    for copy in copies:
        copy.start()
    for copy in copies:
        copy.wait()
    narrow, rows = image_ref.shape
    image, text = rows_first(image_ref[...]), rows_first(text_ref[...])
    blocks_i, blocks_j = rows // of_i // SUB, rows // of_j // 2 // SUB

    def block(rows_of, index):
        value = rows_of[index * SUB : (index + 1) * SUB]
        return (lambda which: value, 0)

    for j in range(of_j):
        for i in range(of_i):
            texts = [block(text, (j * 2 + i % 2) * blocks_j + k) for k in range(blocks_j)]
            images = [block(image, i * blocks_i + k) for k in range(blocks_i)]
            for which, value in enumerate(packed(images + texts, narrow)):
                out_ref[j * of_i + i, :, which * LANES : (which + 1) * LANES] = value


def side_by_side(groups, full, rest):
    found, shared, per = [], [], LANES // rest
    for group, tiles in enumerate(groups):
        found += [((group * full + which) * LANES, tiles[which]) for which in range(full)]
        at = group % per * rest
        moved = shift(tiles[full], at)
        if at == 0:
            shared.append(moved)
        else:
            shared[-1] = jnp.where(lanes_from(at, moved.shape), moved, shared[-1])
    return found + [((len(groups) * full + k) * LANES, tile) for k, tile in enumerate(shared)]


def apart(ref, groups, full, rest):
    per = LANES // rest
    found = []
    for group in range(groups):
        tiles = [ref[:, (group * full + k) * LANES : (group * full + k + 1) * LANES] for k in range(full)]
        lo = (groups * full + group // per) * LANES
        found.append(tiles + [shift(ref[:, lo : lo + LANES], -(group % per) * rest)])
    return found


def widen_kernel(sizes, narrow, got_ref, image_ref, text_ref):
    of_i, of_j, blocks_i, blocks_j = sizes
    copies = image_ref.shape[0]
    full, rest = divmod(of_i * narrow, LANES)
    last, texts = None, []
    for j in range(of_j):
        sources = [reader(got_ref, j * of_i + i) for i in range(of_i)]
        for k in range(blocks_i + blocks_j):
            tiles = packed([(source, k * narrow) for source in sources], narrow)
            if k < blocks_i:
                group = j * blocks_i + k
                for copy in range(copies):
                    for which in range(full):
                        lo = (group * full + which) * LANES
                        image_ref[copy, :, lo : lo + LANES] = tiles[which]
                moved = shift(tiles[full], group * rest)
                last = moved if last is None else jnp.where(lanes_from(group * rest, moved.shape), moved, last)
            else:
                texts.append(tiles)
    for lane, value in side_by_side(texts, full, rest):
        text_ref[:, lane : lane + LANES] = value
    lo = of_j * blocks_i * full * LANES
    for copy in range(copies):
        image_ref[copy, :, lo : lo + LANES] = last


def stacked(image_ref, groups, full, rest):
    sources = image_ref.shape[0]
    lo = groups * full * LANES
    last = image_ref[:, :, lo : lo + LANES].reshape(sources * SUB, LANES)
    found = []
    for group in range(groups):
        at = group * full * LANES
        whole = image_ref[:, :, at : at + full * LANES].reshape(sources * SUB, full * LANES)
        found.append(jnp.concatenate([whole, shift(last, -group * rest)], axis=1))
    return jnp.concatenate(found, axis=0)


dot = functools.partial(
    lax.dot_general, preferred_element_type=jnp.float32, precision=lax.Precision.HIGHEST
)


def both_halves(tiling, text_ref, pair_ref):
    groups, full, rest = tiling
    rows = []
    for ref in (text_ref, pair_ref):
        for tiles in apart(ref, groups, full, rest):
            last = jnp.where(lanes_from(rest, tiles[full].shape), 0.0, tiles[full])
            rows.append(jnp.concatenate(tiles[:full] + [last], axis=1))
    return jnp.concatenate(rows, axis=0)


def logits_kernel(tiling, text_tiling, image_ref, text_ref, pair_ref, out_ref):
    text = both_halves(text_tiling, text_ref, pair_ref)
    out_ref[...] = dot(stacked(image_ref, *tiling), text, (((1,), (1,)), ((), ())))


def image_grads_kernel(sizes, tiling, text_tiling, log_scale_ref, bias_ref, both_ref, text_ref, pair_ref, gi_ref, coef_ref):
    high, of_y, rows, group_i, group_j = sizes
    groups, full, rest = tiling
    sources = gi_ref.shape[0]
    scale = jnp.exp(jnp.full((1, 1), log_scale_ref[0], jnp.float32))
    logits = scale * (both_ref[0] + both_ref[1]) + bias_ref[0]
    x, y, i, j = (lax.axis_index(a) for a in ("x", "y", "zm", "zh"))
    r = lax.broadcasted_iota(jnp.int32, logits.shape, 0)
    group, source = r // (sources * SUB), r % (sources * SUB) // SUB
    blocks_i = group_i // SUB
    zh, inner = group // blocks_i, group % blocks_i * SUB + r % SUB
    row_ids = ((source // of_y * high + zh) * of_y + source % of_y) * rows + i * group_i + inner
    c = lax.broadcasted_iota(jnp.int32, logits.shape, 1)
    half, of_half = group_j // 2, logits.shape[1] // 2
    which = (i + c // of_half) % 2
    zh, inner = c % of_half // half, c % half
    col_ids = ((x * high + zh) * of_y + y) * rows + j * group_j + which * half + inner
    label = jnp.where(row_ids == col_ids, 1.0, -1.0)
    coef = -label * jax.nn.sigmoid(-label * logits)
    coef = scale * coef
    coef_ref[...] = coef
    found = dot(coef, both_halves(text_tiling, text_ref, pair_ref), (((1,), (0,)), ((), ())))
    last = None
    for group in range(groups):
        part = found[group * sources * SUB : (group + 1) * sources * SUB]
        at = group * full * LANES
        gi_ref[:, :, at : at + full * LANES] = part[:, : full * LANES].reshape(sources, SUB, full * LANES)
        moved = shift(part[:, full * LANES :], group * rest)
        last = moved if last is None else last + moved
    lo = groups * full * LANES
    gi_ref[:, :, lo : lo + LANES] = last.reshape(sources, SUB, LANES)


def text_grads_kernel(tiling, coef_ref, image_ref, gt_ref, gt_pair_ref):
    _, full, rest = tiling
    of_half = gt_ref.shape[0]
    found = dot(coef_ref[...], stacked(image_ref, *tiling), (((0,), (0,)), ((), ())))
    gt_ref[...] = found[:of_half]
    pair = [found[at : at + SUB] for at in range(of_half, 2 * of_half, SUB)]
    pair = [[rows_of[:, k * LANES : (k + 1) * LANES] for k in range(full + 1)] for rows_of in pair]
    for lane, value in side_by_side(pair, full, rest):
        gt_pair_ref[:, lane : lane + LANES] = value


def narrow_kernel(sizes, narrow, image_ref, text_ref, pair_ref, out_ref):
    of_i, of_j, blocks_i, blocks_j = sizes
    full, rest = divmod(of_i * narrow, LANES)
    total = image_ref[0]
    for copy in range(1, image_ref.shape[0]):
        total = total + image_ref[copy]
    lo = of_j * blocks_i * full
    tiles = [total[:, k * LANES : (k + 1) * LANES] for k in range(lo + 1)]

    def image_row(group):
        row = tiles[group * full : (group + 1) * full] + [shift(tiles[lo], -group * rest)]
        return lambda which: row[which]

    pair = apart(pair_ref, of_j * blocks_j, full, rest)

    def text_row(start):
        own = reader(text_ref, None, start)
        row = [own(which) + pair[start // SUB][which] for which in range(full + 1)]
        return lambda which: row[which]

    for j in range(of_j):
        rows = [image_row(j * blocks_i + k) for k in range(blocks_i)]
        rows += [text_row((j * blocks_j + k) * SUB) for k in range(blocks_j)]
        for i in range(of_i):
            for which, value in enumerate(packed([(row, i * narrow) for row in rows], narrow)):
                out_ref[j * of_i + i, :, which * LANES : (which + 1) * LANES] = value


def collect_kernel(sizes, got_ref, image_ref, text_ref):
    of_i, of_j, blocks_i, blocks_j = sizes
    narrow = image_ref.shape[0]

    def total(sources, first, last):
        tiles = {}
        for which in range(first * narrow // LANES, tiles_of(last * narrow)):
            tiles[which] = reader(got_ref, sources[0])(which)
            for source in sources[1:]:
                tiles[which] = tiles[which] + reader(got_ref, source)(which)
        return [pick(lambda which: tiles[which], k * narrow, narrow, 0) for k in range(first, last)]

    images, texts = [], []
    for i in range(of_i):
        images += total([j * of_i + i for j in range(of_j)], 0, blocks_i)
    for j in range(of_j):
        for half in range(2):
            texts += total([j * of_i + i for i in range(half, of_i, 2)], blocks_i, blocks_i + blocks_j)
    image_ref[...] = jnp.concatenate(images, axis=0).T[:narrow]
    text_ref[...] = jnp.concatenate(texts, axis=0).T[:narrow]


def call(kernel, outs, *operands, inputs=None, scratch=()):
    many = isinstance(outs, list)
    shapes = [jax.ShapeDtypeStruct(s, jnp.float32) for s in (outs if many else [outs])]
    return pl.pallas_call(
        kernel,
        out_shape=shapes if many else shapes[0],
        in_specs=inputs or [VMEM] * len(operands),
        out_specs=[VMEM] * len(shapes) if many else VMEM,
        scratch_shapes=list(scratch),
        compiler_params=pltpu.CompilerParams(vmem_limit_bytes=32 * 1024 * 1024),
    )(*operands)


def exchange(value, axis):
    return lax.all_to_all(value, axis, split_axis=0, concat_axis=0, tiled=True)


def on_device(image_emb, text_emb, log_scale, logit_bias):
    of_x, of_j, of_y, of_i = (lax.axis_size(a) for a in ("x", "zh", "y", "zm"))
    rows, narrow = image_emb.shape
    group_i, group_j = rows // of_i, rows // of_j
    blocks = (of_i, of_j, group_i // SUB, group_j // 2 // SUB)
    full, rest = divmod(of_i * narrow, LANES)
    groups = of_j * blocks[2]
    assert 0 < rest * groups <= LANES
    tiling = (groups, full, rest)
    plane = of_x * of_y
    text_groups = of_j * blocks[3]
    text_tiling = (text_groups, full, rest)
    text_shape = (SUB, (text_groups * full + -(-text_groups // (LANES // rest))) * LANES)
    grad_shape = (text_groups * SUB, (full + 1) * LANES)
    sent_shape = (of_j * of_i, SUB, tiles_of((blocks[2] + blocks[3]) * narrow) * LANES)
    block = pltpu.VMEM((narrow, rows), jnp.float32)

    held = [pltpu.with_memory_space_constraint(a.T, pltpu.HBM) for a in (image_emb, text_emb)]
    sent = call(
        functools.partial(split_kernel, of_i, of_j), sent_shape, *held,
        inputs=[pl.BlockSpec(memory_space=pltpu.HBM)] * 2,
        scratch=[block, block, pltpu.SemaphoreType.DMA((2,))],
    )
    got = exchange(sent, ("zh", "zm"))
    mine, text = call(
        functools.partial(widen_kernel, blocks, narrow),
        [(plane, SUB, (groups * full + 1) * LANES), text_shape],
        got,
    )
    pairs = [(k, k ^ 1) for k in range(of_i)]
    pair = lax.ppermute(text, "zm", pairs)
    image = exchange(mine, ("x", "y"))
    part = call(functools.partial(logits_kernel, tiling, text_tiling), (plane * groups * SUB, of_j * group_j), image, text, pair)
    other = lax.ppermute(part, "ze", [(0, 1), (1, 0)])
    both = lax.all_gather(part + other, "c")
    grad_i, coef = call(
        functools.partial(image_grads_kernel, (of_j, of_y, rows, group_i, group_j), tiling, text_tiling),
        [image.shape, part.shape],
        log_scale, logit_bias, both, text, pair,
        inputs=[SMEM] * 2 + [VMEM] * 3,
    )
    grad_t, grad_pair = call(functools.partial(text_grads_kernel, tiling), [grad_shape, text_shape], coef, image)
    back_t = lax.ppermute(grad_pair, "zm", pairs)
    back = exchange(grad_i, ("x", "y"))
    sent = call(functools.partial(narrow_kernel, blocks, narrow), sent_shape, back, grad_t, back_t)
    got = exchange(sent, ("zh", "zm"))
    out_i, out_t = call(functools.partial(collect_kernel, blocks), [(narrow, rows), (narrow, rows)], got)
    return (out_i.T, out_t.T)


def program(mesh, sizes):
    x, zh, y, zl, c = sizes
    fine = Mesh(mesh.devices.reshape(x, zh, y, zl // 2, 2, c), ("x", "zh", "y", "zm", "ze", "c"))
    dp, mp = ("x", "zh", "y"), ("zm", "ze", "c")
    return jax.shard_map(
        on_device,
        mesh=fine,
        in_specs=(P(dp, mp), P(dp, mp), P(), P()),
        out_specs=(P(dp, mp), P(dp, mp)),
        check_vma=False,
    )


def solution(mesh):
    return program(mesh, (4, 2, 4, 16, 2))
```
